512 devices in a mesh: pair: 16 (over y, z_lo), row: 32 (over z_hi, x, core).
Axes of the slice: x: 4, y: 4, z: 16 (z_hi: 4, z_lo: 4; z = z_hi * 4 + z_lo), core: 2. Of those that a mesh axis runs over, the one named last changes fastest.
Arguments:
- matrix: float32 [65536, 4096], P('row', 'pair'), may hold values from -500 to 500, as said below
Outputs:
- rotated: float32 [65536, 4096], P('row', 'pair')
The draws below stay inside these ranges and needn't reach their ends.
Inputs may be any that keep to these rules, and one draw needn't show every extreme that they name: Real entries of the matrix.
All inputs are finite; a program needn't handle non-finite values.
Results may differ from the reference program's by a relative error of at most 0.0003.
Values sent between devices are 32-bit elements; how exact they have to be, the bound alone decides.
A program may use at most 64 MiB of HBM per device.

```python
import math
import jax
import jax.numpy as jnp
import numpy as np
from jax import lax

BLOCK = 128
ROUNDS = 128
STEPS = 1
ROWS = 65536
COLS = 4096
N_PAIR = 16


def draw_matrix(key, part):
    key = jax.random.fold_in(key, 11)
    rough_key, row_key, col_key, left_key, right_key = jax.random.split(key, 5)
    position = jnp.arange(ROWS, dtype=jnp.float32) / ROWS
    block_parity = jnp.arange(COLS, dtype=jnp.int32) // BLOCK % 2
    rough_part = jax.random.truncated_normal(rough_key, -3.0, 3.0, (ROWS, COLS), jnp.float32)
    row_scale = jnp.exp(jax.random.uniform(row_key, (ROWS,), jnp.float32, math.log(0.3), math.log(3.0)) + 0.5 * math.log(3.0) * position)
    row_factor = jax.random.truncated_normal(left_key, -3.0, 3.0, (ROWS, 3), jnp.float32)
    col_factor = 0.3 * jax.random.truncated_normal(right_key, -2.0, 2.0, (3, COLS), jnp.float32)
    unit_spread = jax.random.uniform(col_key, (COLS,), jnp.float32, 0.0, math.log(2.0))
    low_scale = jnp.exp(math.log(0.175) + unit_spread)
    high_scale = jnp.exp(unit_spread)
    col_scale = jnp.where(block_parity == 0, low_scale, high_scale)
    common = row_factor[:, 0:1] * col_factor[0:1, :] + row_factor[:, 1:2] * col_factor[1:2, :] + row_factor[:, 2:3] * col_factor[2:3, :]
    return (row_scale[:, None] * col_scale[None, :] * (rough_part + common)).astype(jnp.float32)


def setup_inputs(seed: int = 0) -> dict:
    key_of = jax.random.split(jax.random.key(seed), 2)
    return {
        "matrix": draw_matrix(jax.random.fold_in(key_of[1], 71), 0),
    }


def roll_half(values, offset, along_axis):
    half_size = values.shape[along_axis] // 2
    first_half = lax.slice_in_dim(values, 0, half_size, axis=along_axis)
    second_half = lax.slice_in_dim(values, half_size, 2 * half_size, axis=along_axis)
    return jnp.concatenate([first_half, jnp.roll(second_half, offset, axis=along_axis)], axis=along_axis)


def rotate_pairs(values, cosine, sine_part, along_axis):
    half_size = values.shape[along_axis] // 2
    first_half = lax.slice_in_dim(values, 0, half_size, axis=along_axis)
    second_half = lax.slice_in_dim(values, half_size, 2 * half_size, axis=along_axis)
    if along_axis == 0:
        cosine = cosine[:, None]
        sine_part = sine_part[:, None]
    new_first = first_half * cosine - second_half * sine_part
    new_second = first_half * sine_part + second_half * cosine
    return jnp.concatenate([new_first, new_second], axis=along_axis)


def jacobi_rounds(gram_pair):
    full_size = gram_pair.shape[0]
    half_size = full_size // 2
    mixing = jnp.eye(full_size, dtype=gram_pair.dtype)

    def one_round(round_index, carry):
        gram_now, mixing_now = carry
        alpha_norm = jnp.diagonal(gram_now[:half_size, :half_size])
        beta_norm = jnp.diagonal(gram_now[half_size:, half_size:])
        gamma_cross = jnp.diagonal(gram_now[:half_size, half_size:])
        spread = beta_norm - alpha_norm
        half_angle = 0.5 * jnp.arctan2(2.0 * gamma_cross * jnp.sign(spread), jnp.abs(spread))
        cosine = jnp.cos(half_angle)
        sine_part = jnp.sin(half_angle)
        gram_now = rotate_pairs(rotate_pairs(gram_now, cosine, sine_part, 1), cosine, sine_part, 0)
        mixing_now = rotate_pairs(mixing_now, cosine, sine_part, 1)
        gram_now = roll_half(roll_half(gram_now, -1, 0), -1, 1)
        mixing_now = roll_half(mixing_now, -1, 1)
        return gram_now, mixing_now

    gram_pair, mixing = lax.fori_loop(0, ROUNDS, one_round, (gram_pair, mixing))
    return roll_half(mixing, ROUNDS % half_size, 1)


def pass_order(pair_count):
    table = np.zeros(2 * pair_count, dtype=np.int32)
    for pair_index in range(pair_count):
        if pair_index == 0:
            table[0] = 0
        elif pair_index == 1:
            table[2] = 1
        else:
            table[2 * pair_index] = 2 * (pair_index - 1)
        if pair_index == pair_count - 1:
            table[2 * pair_index + 1] = 2 * (pair_count - 1)
        else:
            table[2 * pair_index + 1] = 2 * (pair_index + 1) + 1
    return table


def reference(matrix):
    row_count = matrix.shape[0]
    pair_width = 2 * BLOCK
    table = pass_order(N_PAIR)
    blocks = matrix
    for step_index in range(STEPS):
        current = blocks

        def rotate_one(pair_index):
            pair_cols = lax.dynamic_slice_in_dim(current, pair_index * pair_width, pair_width, axis=1)
            gram_pair = lax.dot_general(pair_cols, pair_cols, (((0,), (0,)), ((), ())), precision=lax.Precision.HIGHEST, preferred_element_type=jnp.float32)
            mixing = jacobi_rounds(gram_pair)
            return jnp.dot(pair_cols, mixing, precision=lax.Precision.HIGHEST, preferred_element_type=jnp.float32)

        rotated = lax.map(rotate_one, jnp.arange(N_PAIR, dtype=jnp.int32))
        rotated = jnp.transpose(rotated, (1, 0, 2)).reshape(row_count, 2 * N_PAIR, BLOCK)
        blocks = rotated[:, table, :].reshape(row_count, 2 * N_PAIR * BLOCK)
    return blocks
```

```python
import functools

import jax
import jax.numpy as jnp
from jax import lax
from jax.experimental import pallas as pl
from jax.experimental.pallas import tpu as pltpu
from jax.sharding import PartitionSpec as P

N = 128
D = 72
MESH = pl.DeviceIdType.MESH
HIGH = lax.Precision.HIGHEST


def angles(a, b, g):
    d = b - a
    x = jnp.abs(d)
    y = 2.0 * g
    scale = jnp.where(jnp.maximum(x, jnp.abs(y)) < 2.0**-50, 2.0**80, 1.0)
    x = x * scale
    y = jnp.where(d < 0, -y, y) * scale
    turns = x > 0
    x = jnp.where(turns, x, 1.0)
    y = jnp.where(turns, y, 0.0)
    inv = lax.rsqrt(x * x + y * y)
    c2 = 0.5 + (0.5 * x) * inv
    inv_c = lax.rsqrt(c2)
    return c2 * inv_c, ((0.5 * y) * inv) * inv_c


def fan(x):
    return pltpu.roll(x, 0, 1, stride=1, stride_axis=0)


def fan_back(x):
    row = lax.broadcasted_iota(jnp.int32, x.shape, 0)
    for bit in (1, 2, 4):
        x = jnp.where((row & bit) != 0, pltpu.roll(x, N - bit, 1), x)
    parts = [x[m : m + 8] if m == 0 else pltpu.roll(x[m : m + 8], N - m, 1) for m in range(0, N, 8)]
    return jnp.concatenate(parts, axis=0)


def skew(transposed):
    return fan(fan_back(transposed).T)


def rounds(gram_ref, out_ref, a_ref, b_ref, g_ref, t_ref, ml_ref, mr_ref):
    cross = gram_ref[N : 2 * N]
    a_ref[...] = skew(gram_ref[:N])[:D]
    b_ref[...] = skew(gram_ref[2 * N :])[:D]
    g_ref[pl.ds(N, D), :] = skew(cross.T)[:D]
    t_ref[pl.ds(0, D), :] = skew(cross)[:D]
    ml_ref[...] = jnp.zeros_like(ml_ref)
    mr_ref[...] = jnp.zeros_like(mr_ref)
    ml_ref[0, pl.ds(0, 1), :] = jnp.ones((1, N), jnp.float32)
    mr_ref[1, pl.ds(N, 1), :] = jnp.ones((1, N), jnp.float32)

    def one_round(rows, r, carry):
        c, s = angles(*carry)
        n = max(rows, D)
        cd = fan(jnp.broadcast_to(c, (n, N)))
        sd = fan(jnp.broadcast_to(s, (n, N)))
        a, b = a_ref[...], b_ref[...]
        gw, tw = pl.ds(N - r, D), pl.ds(r, D)
        g, t = g_ref[gw, :], t_ref[tw, :]
        a, t = c * a - s * t, s * a + c * t
        g, b = c * g - s * b, s * g + c * b
        ch, sh = cd[:D], sd[:D]
        a, g = ch * a - sh * g, sh * a + ch * g
        t, b = ch * t - sh * b, sh * t + ch * b
        b = pltpu.roll(b, N - 1, 1)
        t = pltpu.roll(t, N - 1, 1)
        a_ref[...] = a
        b_ref[...] = b
        g_ref[gw, :] = g
        t_ref[tw, :] = t
        g_ref[pl.ds(N - 1 - r, 1), :] = t[1:2]
        t_ref[pl.ds(r + D, 1), :] = pltpu.roll(g[N - D : N - D + 1], D - 1, 1)
        mw = pl.ds(N - r, rows)
        cm, sm = cd[:rows], sd[:rows]
        for h in range(2):
            left, right = ml_ref[h, pl.ds(0, rows), :], mr_ref[h, mw, :]
            ml_ref[h, pl.ds(0, rows), :] = cm * left - sm * right
            mr_ref[h, mw, :] = sm * left + cm * right
        return a[0:1], b[0:1], t[1:2]

    carry = (a_ref[0:1, :], b_ref[0:1, :], t_ref[0:1, :])
    stages = 4
    for stage in range(stages):
        first, last = N * stage // stages, N * (stage + 1) // stages
        carry = lax.fori_loop(first, last, functools.partial(one_round, last), carry)
    for h in range(2):
        mr_ref[h, pl.ds(0, 1), :] = mr_ref[h, pl.ds(N, 1), :]
        out_ref[0:N, h * N : (h + 1) * N] = fan(fan_back(ml_ref[h]).T)
        out_ref[N:, h * N : (h + 1) * N] = fan(fan_back(mr_ref[h, 0:N, :]).T)


ROUND_SCRATCH = [
    pltpu.VMEM((D, N), jnp.float32),
    pltpu.VMEM((D, N), jnp.float32),
    pltpu.VMEM((208, N), jnp.float32),
    pltpu.VMEM((208, N), jnp.float32),
    pltpu.VMEM((2, N, N), jnp.float32),
    pltpu.VMEM((2, 2 * N, N), jnp.float32),
]


def gram_kernel(x_ref, sum_ref, part, half, piece, in_core, in_x, in_z, send, recv_core, recv_x, recv_z, recv_gx, recv_gc):
    me = lax.axis_index("row")
    core, x, z = lax.rem(me, 2), lax.rem(me // 2, 4), me // 8

    def place(z, x, core):
        return {"row": (z * 4 + x) * 2 + core}

    barrier = pltpu.get_barrier_semaphore()
    pl.semaphore_signal(barrier, inc=1, device_id=place(z, x, 1 - core), device_id_type=MESH)
    for k in range(1, 4):
        pl.semaphore_signal(barrier, inc=1, device_id=place(z, lax.rem(x + k, 4), core), device_id_type=MESH)
        pl.semaphore_signal(barrier, inc=1, device_id=place(lax.rem(z + k, 4), x, core), device_id_type=MESH)

    left, right = x_ref[:, :N], x_ref[:, N:]

    def cross(u, v):
        return lax.dot_general(u, v, (((0,), (0,)), ((), ())), precision=HIGH, preferred_element_type=jnp.float32)

    part[:N] = cross(left, left)
    part[N : 2 * N] = cross(left, right)
    part[2 * N :] = cross(right, right)
    pl.semaphore_wait(barrier, 7)

    def copy(src, dst, send_sem, recv_sem, to):
        return pltpu.make_async_remote_copy(
            src_ref=src, dst_ref=dst, send_sem=send_sem, recv_sem=recv_sem, device_id=to, device_id_type=MESH
        )

    h = 3 * N // 2
    q = h // 4
    mine = pl.ds(pl.multiple_of(core * h, 8), h)
    other = pl.ds(pl.multiple_of((1 - core) * h, 8), h)
    sent = []
    c = copy(part.at[other], in_core, send.at[0], recv_core, place(z, x, 1 - core))
    c.start()
    sent.append(c)
    c.wait_recv()
    half[...] = part[mine] + in_core[...]

    quarter = pl.ds(pl.multiple_of(x * q, 8), q)
    for k in range(1, 4):
        xt = lax.rem(x + k, 4)
        c = copy(half.at[pl.ds(pl.multiple_of(xt * q, 8), q)], in_x.at[x], send.at[k], recv_x.at[x], place(z, xt, core))
        c.start()
        sent.append(c)
    in_x[x] = half[quarter]
    for k in range(1, 4):
        xf = lax.rem(x + k, 4)
        copy(in_x.at[xf], in_x.at[xf], send.at[k], recv_x.at[xf], place(z, xf, core)).wait_recv()
    in_z[z] = (in_x[0] + in_x[1]) + (in_x[2] + in_x[3])

    for k in range(1, 4):
        zt = lax.rem(z + k, 4)
        c = copy(in_z.at[z], in_z.at[z], send.at[3 + k], recv_z.at[z], place(zt, x, core))
        c.start()
        sent.append(c)
    for k in range(1, 4):
        zf = lax.rem(z + k, 4)
        copy(in_z.at[zf], in_z.at[zf], send.at[3 + k], recv_z.at[zf], place(zf, x, core)).wait_recv()

    def rows_of(core, x):
        return pl.ds(pl.multiple_of(core * h + x * q, 8), q)

    own = sum_ref.at[rows_of(core, x)]
    own[...] = (in_z[0] + in_z[1]) + (in_z[2] + in_z[3])
    for k in range(1, 4):
        c = copy(own, own, send.at[6 + k], recv_gx.at[x], place(z, lax.rem(x + k, 4), core))
        c.start()
        sent.append(c)
    for k in range(4):
        xf = lax.rem(x + k, 4)
        there = sum_ref.at[rows_of(core, xf)]
        if k:
            copy(there, there, send.at[6 + k], recv_gx.at[xf], place(z, xf, core)).wait_recv()
        c = copy(there, there, send.at[10 + k], recv_gc.at[xf], place(z, x, 1 - core))
        c.start()
        sent.append(c)
    for k in range(4):
        xf = lax.rem(x + k, 4)
        there = sum_ref.at[rows_of(1 - core, xf)]
        copy(there, there, send.at[10 + k], recv_gc.at[xf], place(z, x, 1 - core)).wait_recv()
    for c in sent:
        c.wait_send()


def summed_gram(x):
    q = 3 * N // 8
    dma = pltpu.SemaphoreType.DMA
    return pl.pallas_call(
        gram_kernel,
        out_shape=jax.ShapeDtypeStruct((3 * N, N), jnp.float32),
        in_specs=[pl.BlockSpec(memory_space=pltpu.VMEM)],
        out_specs=pl.BlockSpec(memory_space=pltpu.VMEM),
        scratch_shapes=[
            pltpu.VMEM((3 * N, N), jnp.float32),
            pltpu.VMEM((4 * q, N), jnp.float32),
            pltpu.VMEM((q, N), jnp.float32),
            pltpu.VMEM((4 * q, N), jnp.float32),
            pltpu.VMEM((4, q, N), jnp.float32),
            pltpu.VMEM((4, q, N), jnp.float32),
            dma((14,)),
            dma,
            dma((4,)),
            dma((4,)),
            dma((4,)),
            dma((4,)),
        ],
        compiler_params=pltpu.CompilerParams(collective_id=0, has_side_effects=True, vmem_limit_bytes=40 << 20),
        name="gram_sum",
    )(x)


def jacobi_rounds(gram):
    return pl.pallas_call(
        rounds,
        out_shape=jax.ShapeDtypeStruct((2 * N, 2 * N), jnp.float32),
        in_specs=[pl.BlockSpec(memory_space=pltpu.VMEM)],
        out_specs=pl.BlockSpec(memory_space=pltpu.VMEM),
        scratch_shapes=ROUND_SCRATCH,
        compiler_params=pltpu.CompilerParams(vmem_limit_bytes=40 << 20),
        name="jacobi_rounds",
    )(gram)


CHUNKS = 8


def move_kernel(x_ref, m_ref, out_ref, y, send_f, send_b, recv_f, recv_b, local):
    k = lax.axis_index("pair")
    last = lax.axis_size("pair") - 1
    barrier = pltpu.get_barrier_semaphore()
    after, before = lax.rem(k + 1, last + 1), lax.rem(k + last, last + 1)
    for to in (after, before):
        pl.semaphore_signal(barrier, inc=1, device_id={"pair": to}, device_id_type=MESH)
    pl.semaphore_wait(barrier, 2)
    rows = x_ref.shape[0] // CHUNKS

    def forward(j):
        at = pl.ds(j * rows, rows)
        return pltpu.make_async_remote_copy(
            src_ref=y.at[jnp.where(k == 0, 1, 0), at], dst_ref=out_ref.at[at, pl.ds(0, N)],
            send_sem=send_f.at[j], recv_sem=recv_f.at[j], device_id={"pair": after}, device_id_type=MESH,
        )

    def backward(j):
        at = pl.ds(j * rows, rows)
        return pltpu.make_async_remote_copy(
            src_ref=y.at[1, at], dst_ref=out_ref.at[at, pl.ds(N, N)],
            send_sem=send_b.at[j], recv_sem=recv_b.at[j], device_id={"pair": before}, device_id_type=MESH,
        )

    keep_left = pltpu.make_async_copy(y.at[0], out_ref.at[:, pl.ds(0, N)], local)
    keep_right = pltpu.make_async_copy(y.at[0], out_ref.at[:, pl.ds(N, N)], local)

    for j in range(CHUNKS):
        at = pl.ds(j * rows, rows)
        moved = lax.dot_general(
            x_ref[at, :], m_ref[...], (((1,), (1,)), ((), ())), precision=HIGH, preferred_element_type=jnp.float32
        )
        y[0, at] = moved[:, :N]
        y[1, at] = moved[:, N:]
        pl.when(k < last)(lambda: forward(j).start())
        pl.when(k > 0)(lambda: backward(j).start())
    pl.when(k == 0)(lambda: keep_left.start())
    pl.when(k == last)(lambda: keep_right.start())
    for j in range(CHUNKS):
        pl.when(k < last)(lambda: forward(j).wait_send())
        pl.when(k > 0)(lambda: backward(j).wait_send())
        pl.when(k > 0)(lambda: forward(j).wait_recv())
        pl.when(k < last)(lambda: backward(j).wait_recv())
    pl.when(k == 0)(lambda: keep_left.wait())
    pl.when(k == last)(lambda: keep_right.wait())


def mixed_and_moved(x, mixing):
    dma = pltpu.SemaphoreType.DMA
    return pl.pallas_call(
        move_kernel,
        out_shape=jax.ShapeDtypeStruct(x.shape, jnp.float32),
        in_specs=[pl.BlockSpec(memory_space=pltpu.VMEM)] * 2,
        out_specs=pl.BlockSpec(memory_space=pl.ANY),
        scratch_shapes=[pltpu.VMEM((2, x.shape[0], N), jnp.float32)] + [dma((CHUNKS,))] * 4 + [dma],
        compiler_params=pltpu.CompilerParams(collective_id=1, has_side_effects=True, vmem_limit_bytes=40 << 20),
        name="mix_and_move",
    )(x, mixing)


def per_device(matrix):
    return mixed_and_moved(matrix, jacobi_rounds(summed_gram(matrix)))


def solution(mesh):
    return jax.shard_map(
        per_device, mesh=mesh, in_specs=(P("row", "pair"),), out_specs=P("row", "pair"), check_vma=False
    )
```

```python
import functools

import jax
import jax.numpy as jnp
from jax import lax
from jax.experimental import pallas as pl
from jax.experimental.pallas import tpu as pltpu
from jax.sharding import PartitionSpec as P

N = 128
D = 72
MESH = pl.DeviceIdType.MESH
HIGH = lax.Precision.HIGHEST


def angles(a, b, g):
    d = b - a
    x = jnp.abs(d)
    y = 2.0 * g
    scale = jnp.where(jnp.maximum(x, jnp.abs(y)) < 2.0**-50, 2.0**80, 1.0)
    x = x * scale
    y = jnp.where(d < 0, -y, y) * scale
    turns = x > 0
    x = jnp.where(turns, x, 1.0)
    y = jnp.where(turns, y, 0.0)
    inv = lax.rsqrt(x * x + y * y)
    c2 = 0.5 + (0.5 * x) * inv
    inv_c = lax.rsqrt(c2)
    return c2 * inv_c, ((0.5 * y) * inv) * inv_c


def fan(x):
    return pltpu.roll(x, 0, 1, stride=1, stride_axis=0)


def fan_back(x):
    row = lax.broadcasted_iota(jnp.int32, x.shape, 0)
    for bit in (1, 2, 4):
        x = jnp.where((row & bit) != 0, pltpu.roll(x, N - bit, 1), x)
    parts = [x[m : m + 8] if m == 0 else pltpu.roll(x[m : m + 8], N - m, 1) for m in range(0, N, 8)]
    return jnp.concatenate(parts, axis=0)


def skew(transposed):
    return fan(fan_back(transposed).T)


def rounds(gram_ref, out_ref, a_ref, b_ref, g_ref, t_ref, ml_ref, mr_ref):
    cross = gram_ref[N : 2 * N]
    a_ref[...] = skew(gram_ref[:N])[:D]
    b_ref[...] = skew(gram_ref[2 * N :])[:D]
    g_ref[pl.ds(N, D), :] = skew(cross.T)[:D]
    t_ref[pl.ds(0, D), :] = skew(cross)[:D]
    ml_ref[...] = jnp.zeros_like(ml_ref)
    mr_ref[...] = jnp.zeros_like(mr_ref)
    ml_ref[0, pl.ds(0, 1), :] = jnp.ones((1, N), jnp.float32)
    mr_ref[1, pl.ds(N, 1), :] = jnp.ones((1, N), jnp.float32)

    def one_round(rows, r, carry):
        c, s = angles(*carry)
        n = max(rows, D)
        cd = fan(jnp.broadcast_to(c, (n, N)))
        sd = fan(jnp.broadcast_to(s, (n, N)))
        a, b = a_ref[...], b_ref[...]
        gw, tw = pl.ds(N - r, D), pl.ds(r, D)
        g, t = g_ref[gw, :], t_ref[tw, :]
        a, t = c * a - s * t, s * a + c * t
        g, b = c * g - s * b, s * g + c * b
        ch, sh = cd[:D], sd[:D]
        a, g = ch * a - sh * g, sh * a + ch * g
        t, b = ch * t - sh * b, sh * t + ch * b
        b = pltpu.roll(b, N - 1, 1)
        t = pltpu.roll(t, N - 1, 1)
        a_ref[...] = a
        b_ref[...] = b
        g_ref[gw, :] = g
        t_ref[tw, :] = t
        g_ref[pl.ds(N - 1 - r, 1), :] = t[1:2]
        t_ref[pl.ds(r + D, 1), :] = pltpu.roll(g[N - D : N - D + 1], D - 1, 1)
        mw = pl.ds(N - r, rows)
        cm, sm = cd[:rows], sd[:rows]
        for h in range(2):
            left, right = ml_ref[h, pl.ds(0, rows), :], mr_ref[h, mw, :]
            ml_ref[h, pl.ds(0, rows), :] = cm * left - sm * right
            mr_ref[h, mw, :] = sm * left + cm * right
        return a[0:1], b[0:1], t[1:2]

    carry = (a_ref[0:1, :], b_ref[0:1, :], t_ref[0:1, :])
    stages = 4
    for stage in range(stages):
        first, last = N * stage // stages, N * (stage + 1) // stages
        carry = lax.fori_loop(first, last, functools.partial(one_round, last), carry)
    for h in range(2):
        mr_ref[h, pl.ds(0, 1), :] = mr_ref[h, pl.ds(N, 1), :]
        out_ref[0:N, h * N : (h + 1) * N] = fan(fan_back(ml_ref[h]).T)
        out_ref[N:, h * N : (h + 1) * N] = fan(fan_back(mr_ref[h, 0:N, :]).T)


ROUND_SCRATCH = [
    pltpu.VMEM((D, N), jnp.float32),
    pltpu.VMEM((D, N), jnp.float32),
    pltpu.VMEM((208, N), jnp.float32),
    pltpu.VMEM((208, N), jnp.float32),
    pltpu.VMEM((2, N, N), jnp.float32),
    pltpu.VMEM((2, 2 * N, N), jnp.float32),
]


EARLY = 640
RAW_PARTS = 2
RAW_AT = 0
LATE = (128, 128, 256, 256, 256, 384)
STARTS = tuple(EARLY + sum(LATE[:i]) for i in range(len(LATE)))
LOADS = 4


def remote(src, dst, send_sem, recv_sem, to):
    return pltpu.make_async_remote_copy(
        src_ref=src, dst_ref=dst, send_sem=send_sem, recv_sem=recv_sem, device_id=to, device_id_type=MESH
    )


def mixed(rows, mixing):
    return lax.dot_general(
        rows, mixing, (((1,), (1,)), ((), ())), precision=HIGH, preferred_element_type=jnp.float32
    )


def partial_gram(x_ref, xb, part, load):
    size = xb.shape[0] // LOADS
    copies = []
    for j in range(LOADS):
        at = pl.ds(j * size, size)
        copies.append(pltpu.make_async_copy(x_ref.at[at], xb.at[at], load.at[j]))
        copies[-1].start()

    def cross(u, v):
        return lax.dot_general(u, v, (((0,), (0,)), ((), ())), preferred_element_type=jnp.float32)

    even = odd = 0.0
    for j in range(LOADS):
        copies[j].wait()
        x = xb[pl.ds(j * size, size), :]
        high = x.astype(jnp.bfloat16)
        rest = x - high.astype(jnp.float32)
        mid = rest.astype(jnp.bfloat16)
        low = (rest - mid.astype(jnp.float32)).astype(jnp.bfloat16)
        even = even + (cross(high, high) + cross(mid, mid))
        odd = odd + (cross(high, mid) + cross(high, low))
    gram = even + (odd + odd.T)
    part[:N] = gram[:N, :N]
    part[N : 2 * N] = gram[:N, N:]
    part[2 * N :] = gram[N:, N:]


def step_kernel(x_ref, out_ref, xb, y, raw, raw_y, part, half, total, in_core, in_x, in_z, mix, near, round_refs, sems):
    me, k = lax.axis_index("row"), lax.axis_index("pair")
    core, x, z = lax.rem(me, 2), lax.rem(me // 2, 4), me // 8
    last = lax.axis_size("pair") - 1
    after, before = lax.rem(k + 1, last + 1), lax.rem(k + last, last + 1)
    load, send, recv_core, recv_x, recv_z, recv_gx, recv_gc, raw_send, raw_recv, mix_send, mix_recv, late_send, late_recv, keep = sems

    def place(z, x, core):
        return {"row": (z * 4 + x) * 2 + core}

    def peer(i):
        other = lax.rem(me + i, 8)
        return other, {"row": z * 8 + other}

    barrier = pltpu.get_barrier_semaphore()
    for i in range(1, 8):
        pl.semaphore_signal(barrier, inc=1, device_id=peer(i)[1], device_id_type=MESH)
    for i in range(1, 4):
        pl.semaphore_signal(barrier, inc=1, device_id=place(lax.rem(z + i, 4), x, core), device_id_type=MESH)
    for to in (after, before):
        pl.semaphore_signal(barrier, inc=1, device_id={"pair": to}, device_id_type=MESH)

    partial_gram(x_ref, xb, part, load)
    pl.semaphore_wait(barrier, 12)

    h = 3 * N // 2
    q = h // 4
    mine = pl.ds(pl.multiple_of(core * h, 8), h)
    other = pl.ds(pl.multiple_of((1 - core) * h, 8), h)
    sent = []
    c = remote(part.at[other], in_core, send.at[0], recv_core, place(z, x, 1 - core))
    c.start()
    sent.append(c)

    size = EARLY // RAW_PARTS
    raw_f, raw_b = [], []
    for j in range(RAW_PARTS):
        at = pl.ds(j * size, size)
        raw_f.append(remote(xb.at[at], raw.at[0, at], raw_send.at[0, j], raw_recv.at[0, j], {"pair": after}))
        raw_b.append(remote(xb.at[at], raw.at[1, at], raw_send.at[1, j], raw_recv.at[1, j], {"pair": before}))

    def start_raw():
        for j in range(RAW_PARTS):
            pl.when(k < last)(raw_f[j].start)
            pl.when(k > 0)(raw_b[j].start)

    if RAW_AT == 0:
        start_raw()
    c.wait_recv()
    half[...] = part[mine] + in_core[...]

    quarter = pl.ds(pl.multiple_of(x * q, 8), q)
    for i in range(1, 4):
        xt = lax.rem(x + i, 4)
        c = remote(half.at[pl.ds(pl.multiple_of(xt * q, 8), q)], in_x.at[x], send.at[i], recv_x.at[x], place(z, xt, core))
        c.start()
        sent.append(c)
    in_x[x] = half[quarter]
    for i in range(1, 4):
        xf = lax.rem(x + i, 4)
        remote(in_x.at[xf], in_x.at[xf], send.at[i], recv_x.at[xf], place(z, xf, core)).wait_recv()
    in_z[z] = (in_x[0] + in_x[1]) + (in_x[2] + in_x[3])

    for i in range(1, 4):
        zt = lax.rem(z + i, 4)
        c = remote(in_z.at[z], in_z.at[z], send.at[3 + i], recv_z.at[z], place(zt, x, core))
        c.start()
        sent.append(c)
    if RAW_AT == 1:
        start_raw()
    for i in range(1, 4):
        zf = lax.rem(z + i, 4)
        remote(in_z.at[zf], in_z.at[zf], send.at[3 + i], recv_z.at[zf], place(zf, x, core)).wait_recv()
    if RAW_AT == 2:
        start_raw()

    def rows_of(core, x):
        return total.at[pl.ds(pl.multiple_of(core * h + x * q, 8), q)]

    own = rows_of(core, x)
    own[...] = (in_z[0] + in_z[1]) + (in_z[2] + in_z[3])
    for i in range(1, 4):
        c = remote(own, own, send.at[6 + i], recv_gx.at[x], place(z, lax.rem(x + i, 4), core))
        c.start()
        sent.append(c)
    for i in range(4):
        xf = lax.rem(x + i, 4)
        there = rows_of(core, xf)
        if i:
            remote(there, there, send.at[6 + i], recv_gx.at[xf], place(z, xf, core)).wait_recv()
        c = remote(there, there, send.at[10 + i], recv_gc.at[xf], place(z, x, 1 - core))
        c.start()
        sent.append(c)
    for i in range(4):
        xf = lax.rem(x + i, 4)
        there = rows_of(1 - core, xf)
        remote(there, there, send.at[10 + i], recv_gc.at[xf], place(z, x, 1 - core)).wait_recv()
    for c in sent:
        c.wait_send()

    rounds(total, mix, *round_refs)

    seat = lax.rem(me, 8)
    share = N // 8

    def eighth(i):
        return pl.ds(pl.multiple_of(i * share, 8), share)

    first = jnp.where(k == 0, N, 0)
    mix_f = remote(
        mix.at[pl.ds(pl.multiple_of(first + seat * share, 8), share)], near.at[0, eighth(seat)],
        mix_send.at[0, 0], mix_recv.at[0, seat], {"pair": after},
    )
    mix_b = remote(
        mix.at[pl.ds(pl.multiple_of(N + seat * share, 8), share)], near.at[1, eighth(seat)],
        mix_send.at[1, 0], mix_recv.at[1, seat], {"pair": before},
    )
    pl.when(k < last)(mix_f.start)
    pl.when(k > 0)(mix_b.start)

    late_f, late_b = [], []
    for j, (start, size) in enumerate(zip(STARTS, LATE)):
        at = pl.ds(start, size)
        late_f.append(remote(y.at[jnp.where(k == 0, 1, 0), at], out_ref.at[at, pl.ds(0, N)], late_send.at[0, j], late_recv.at[0, j], {"pair": after}))
        late_b.append(remote(y.at[1, at], out_ref.at[at, pl.ds(N, N)], late_send.at[1, j], late_recv.at[1, j], {"pair": before}))

    def spread(which):
        for i in range(1, 8):
            to = peer(i)[1]
            remote(near.at[which, eighth(seat)], near.at[which, eighth(seat)], mix_send.at[which, i], mix_recv.at[which, seat], to).start()

    def rotate(at):
        moved = mixed(xb[at, :], mix[...])
        y[0, at] = moved[:, :N]
        y[1, at] = moved[:, N:]

    for j, (start, size) in enumerate(zip(STARTS, LATE)):
        rotate(pl.ds(start, size))
        pl.when(k < last)(late_f[j].start)
        pl.when(k > 0)(late_b[j].start)

    @pl.when(k > 0)
    def _():
        mix_f.wait_recv()
        spread(0)

    @pl.when(k < last)
    def _():
        mix_b.wait_recv()
        spread(1)

    keep_left = pltpu.make_async_copy(y.at[0], out_ref.at[:, pl.ds(0, N)], keep.at[0])
    keep_right = pltpu.make_async_copy(y.at[0], out_ref.at[:, pl.ds(N, N)], keep.at[1])

    @pl.when((k == 0) | (k == last))
    def _():
        rotate(pl.ds(0, EARLY))

    pl.when(k == 0)(keep_left.start)
    pl.when(k == last)(keep_right.start)

    def finish(which, copies):
        for c in copies:
            c.wait_recv()
        for i in range(1, 8):
            there, device = peer(i)
            slot = near.at[which, eighth(there)]
            remote(slot, slot, mix_send.at[which, i], mix_recv.at[which, there], device).wait_recv()
        raw_y[which] = mixed(raw[which], near[which])
        c = pltpu.make_async_copy(raw_y.at[which], out_ref.at[pl.ds(0, EARLY), pl.ds(which * N, N)], keep.at[which])
        c.start()
        for i in range(1, 8):
            slot = near.at[which, eighth(seat)]
            remote(slot, slot, mix_send.at[which, i], mix_recv.at[which, seat], peer(i)[1]).wait_send()

    pl.when(k > 0)(lambda: finish(0, raw_f))
    pl.when(k < last)(lambda: finish(1, raw_b))

    for c in [mix_f] + raw_f + late_f:
        pl.when(k < last)(c.wait_send)
    for c in [mix_b] + raw_b + late_b:
        pl.when(k > 0)(c.wait_send)
    for c in late_f:
        pl.when(k > 0)(c.wait_recv)
    for c in late_b:
        pl.when(k < last)(c.wait_recv)
    early_left = pltpu.make_async_copy(raw_y.at[0], out_ref.at[pl.ds(0, EARLY), pl.ds(0, N)], keep.at[0])
    early_right = pltpu.make_async_copy(raw_y.at[1], out_ref.at[pl.ds(0, EARLY), pl.ds(N, N)], keep.at[1])
    pl.when(k == 0)(keep_left.wait)
    pl.when(k > 0)(early_left.wait)
    pl.when(k == last)(keep_right.wait)
    pl.when(k < last)(early_right.wait)


def per_device(matrix):
    rows = matrix.shape[0]
    q = 3 * N // 8
    dma = pltpu.SemaphoreType.DMA
    f32 = jnp.float32
    return pl.pallas_call(
        step_kernel,
        out_shape=jax.ShapeDtypeStruct(matrix.shape, f32),
        in_specs=[pl.BlockSpec(memory_space=pl.ANY)],
        out_specs=pl.BlockSpec(memory_space=pl.ANY),
        scratch_shapes=[
            pltpu.VMEM((rows, 2 * N), f32),
            pltpu.VMEM((2, rows, N), f32),
            pltpu.VMEM((2, EARLY, 2 * N), f32),
            pltpu.VMEM((2, EARLY, N), f32),
            pltpu.VMEM((3 * N, N), f32),
            pltpu.VMEM((4 * q, N), f32),
            pltpu.VMEM((3 * N, N), f32),
            pltpu.VMEM((4 * q, N), f32),
            pltpu.VMEM((4, q, N), f32),
            pltpu.VMEM((4, q, N), f32),
            pltpu.VMEM((2 * N, 2 * N), f32),
            pltpu.VMEM((2, N, 2 * N), f32),
            ROUND_SCRATCH,
            [
                dma((LOADS,)),
                dma((14,)),
                dma,
                dma((4,)),
                dma((4,)),
                dma((4,)),
                dma((4,)),
                dma((2, RAW_PARTS)),
                dma((2, RAW_PARTS)),
                dma((2, 8)),
                dma((2, 8)),
                dma((2, len(LATE))),
                dma((2, len(LATE))),
                dma((2,)),
            ],
        ],
        compiler_params=pltpu.CompilerParams(collective_id=0, has_side_effects=True, vmem_limit_bytes=48 << 20),
        name="jacobi_step",
    )(matrix)


def solution(mesh):
    return jax.shard_map(
        per_device, mesh=mesh, in_specs=(P("row", "pair"),), out_specs=P("row", "pair"), check_vma=False
    )
```

```python
import functools

import jax
import jax.numpy as jnp
from jax import lax
from jax.experimental import pallas as pl
from jax.experimental.pallas import tpu as pltpu
from jax.sharding import PartitionSpec as P

N = 128
D = 72
STAGES = 8
UNROLL = 8
MESH = pl.DeviceIdType.MESH
HIGH = lax.Precision.HIGHEST


def angles(a, b, g):
    d = b - a
    x = jnp.abs(d)
    y = 2.0 * g
    scale = jnp.where(jnp.maximum(x, jnp.abs(y)) < 2.0**-50, 2.0**80, 1.0)
    x = x * scale
    y = jnp.where(d < 0, -y, y) * scale
    turns = x > 0
    x = jnp.where(turns, x, 1.0)
    y = jnp.where(turns, y, 0.0)
    inv = lax.rsqrt(x * x + y * y)
    c2 = 0.5 + (0.5 * x) * inv
    inv_c = lax.rsqrt(c2)
    return c2 * inv_c, ((0.5 * y) * inv) * inv_c


def fan(x):
    return pltpu.roll(x, 0, 1, stride=1, stride_axis=0)


def fan_back(x):
    row = lax.broadcasted_iota(jnp.int32, x.shape, 0)
    for bit in (1, 2, 4):
        x = jnp.where((row & bit) != 0, pltpu.roll(x, N - bit, 1), x)
    parts = [x[m : m + 8] if m == 0 else pltpu.roll(x[m : m + 8], N - m, 1) for m in range(0, N, 8)]
    return jnp.concatenate(parts, axis=0)


def skew(transposed):
    return fan(fan_back(transposed).T)


def rounds(gram_ref, out_ref, a_ref, b_ref, g_ref, t_ref, ml_ref, mr_ref):
    cross = gram_ref[N : 2 * N]
    a_ref[...] = skew(gram_ref[:N])[:D]
    b_ref[...] = skew(gram_ref[2 * N :])[:D]
    g_ref[pl.ds(N, D), :] = skew(cross.T)[:D]
    t_ref[pl.ds(0, D), :] = skew(cross)[:D]
    ml_ref[...] = jnp.zeros_like(ml_ref)
    mr_ref[...] = jnp.zeros_like(mr_ref)
    ml_ref[0, pl.ds(0, 1), :] = jnp.ones((1, N), jnp.float32)
    mr_ref[1, pl.ds(N, 1), :] = jnp.ones((1, N), jnp.float32)

    def back(x, lanes):
        return pltpu.roll(x, N - lanes, 1)

    def one_round(rows, r, carry):
        da, db, dg, ea, eb, eg, a1, t1, g1, b1 = carry
        c, s = angles(da, db, dg)
        ce, se = back(c, 1), back(s, 1)
        na = c * (c * da - s * dg) - s * (c * dg - s * db)
        nb = se * (se * ea + ce * eg) + ce * (se * eg + ce * eb)
        ng = c * (se * a1 + ce * t1) - s * (se * g1 + ce * b1)
        n = max(rows, D)
        cd = fan(jnp.broadcast_to(c, (n, N)))
        sd = fan(jnp.broadcast_to(s, (n, N)))
        a, b = a_ref[...], b_ref[...]
        gw, tw = pl.ds(N - r, D), pl.ds(r, D)
        g, t = g_ref[gw, :], t_ref[tw, :]
        a, t = c * a - s * t, s * a + c * t
        g, b = c * g - s * b, s * g + c * b
        ch, sh = cd[:D], sd[:D]
        a, g = ch * a - sh * g, sh * a + ch * g
        t, b = ch * t - sh * b, sh * t + ch * b
        ahead = (back(na, 1), back(nb, 1), back(ng, 1), back(a[1:2], 1), back(t[2:3], 2), back(g[0:1], 1), back(b[1:2], 2))
        b = back(b, 1)
        t = back(t, 1)
        a_ref[...] = a
        b_ref[...] = b
        g_ref[gw, :] = g
        t_ref[tw, :] = t
        g_ref[pl.ds(N - 1 - r, 1), :] = t[1:2]
        t_ref[pl.ds(r + D, 1), :] = back(g[N - D : N - D + 1], N - D + 1)
        mw = pl.ds(N - r, rows)
        cm, sm = cd[:rows], sd[:rows]
        for h in range(2):
            left, right = ml_ref[h, pl.ds(0, rows), :], mr_ref[h, mw, :]
            ml_ref[h, pl.ds(0, rows), :] = cm * left - sm * right
            mr_ref[h, mw, :] = sm * left + cm * right
        return (na, nb, ng) + ahead

    def group(rows, i, carry):
        for u in range(UNROLL):
            carry = one_round(rows, UNROLL * i + u, carry)
        return carry

    first = (a_ref[0:1, :], b_ref[0:1, :], t_ref[0:1, :])
    carry = first + tuple(back(v, 1) for v in first + (a_ref[1:2, :], t_ref[1:2, :], g_ref[N + 1 : N + 2, :], b_ref[1:2, :]))
    for stage in range(STAGES):
        begin, end = N * stage // STAGES, N * (stage + 1) // STAGES
        carry = lax.fori_loop(begin // UNROLL, end // UNROLL, functools.partial(group, end), carry)
    for h in range(2):
        mr_ref[h, pl.ds(0, 1), :] = mr_ref[h, pl.ds(N, 1), :]
        out_ref[0:N, h * N : (h + 1) * N] = fan(fan_back(ml_ref[h]).T)
        out_ref[N:, h * N : (h + 1) * N] = fan(fan_back(mr_ref[h, 0:N, :]).T)


ROUND_SCRATCH = [
    pltpu.VMEM((D, N), jnp.float32),
    pltpu.VMEM((D, N), jnp.float32),
    pltpu.VMEM((208, N), jnp.float32),
    pltpu.VMEM((208, N), jnp.float32),
    pltpu.VMEM((2, N, N), jnp.float32),
    pltpu.VMEM((2, 2 * N, N), jnp.float32),
]


EARLY = 1024
RAW_PARTS = 4
RAW_AT = 2
CHUNK = 256
CHUNKS = 8
QUARTER = CHUNK // 4
ORDER = tuple(range(EARLY // CHUNK, CHUNKS)) + tuple(range(EARLY // CHUNK))
LOADS = 4


def remote(src, dst, send_sem, recv_sem, to):
    return pltpu.make_async_remote_copy(
        src_ref=src, dst_ref=dst, send_sem=send_sem, recv_sem=recv_sem, device_id=to, device_id_type=MESH
    )


def mixed(rows, mixing):
    return lax.dot_general(
        rows, mixing, (((1,), (1,)), ((), ())), precision=HIGH, preferred_element_type=jnp.float32
    )


def partial_gram(x_ref, xb, part, load):
    size = xb.shape[0] // LOADS
    copies = []
    for j in range(LOADS):
        at = pl.ds(j * size, size)
        copies.append(pltpu.make_async_copy(x_ref.at[at], xb.at[at], load.at[j]))
        copies[-1].start()

    def cross(u, v):
        return lax.dot_general(u, v, (((0,), (0,)), ((), ())), preferred_element_type=jnp.float32)

    even = odd = 0.0
    for j in range(LOADS):
        copies[j].wait()
        x = xb[pl.ds(j * size, size), :]
        high = x.astype(jnp.bfloat16)
        rest = x - high.astype(jnp.float32)
        mid = rest.astype(jnp.bfloat16)
        low = (rest - mid.astype(jnp.float32)).astype(jnp.bfloat16)
        even = even + (cross(high, high) + cross(mid, mid))
        odd = odd + (cross(high, mid) + cross(high, low))
    gram = even + (odd + odd.T)
    part[:N] = gram[:N, :N]
    part[N : 2 * N] = gram[:N, N:]
    part[2 * N :] = gram[N:, N:]


def step_kernel(x_ref, out_ref, xb, y, raw, raw_y, relay, part, half, total, in_core, in_x, in_z, mix, near, round_refs, sems):
    me, k = lax.axis_index("row"), lax.axis_index("pair")
    core, x, z = lax.rem(me, 2), lax.rem(me // 2, 4), me // 8
    last = lax.axis_size("pair") - 1
    py, pz = k // 4, lax.rem(k, 4)
    to_after, to_before = pz < 3, pz > 0

    def pair(distance):
        return {"pair": lax.rem(k + distance + last + 1, last + 1)}

    after, before = pair(1), pair(-1)
    top = pz == 3
    edge = top | (pz == 0)
    wraps = (top & (py < 3)) | ((pz == 0) & (py > 0))
    step = jnp.where(top, 1, -1)
    direct_mine = jnp.where(top, 3 - py, py)
    direct_passed = jnp.where(top, 4 - py, py + 1)
    column_mine = pl.ds(pl.multiple_of(jnp.where(top, 0, N), N), N)
    column_here = pl.ds(pl.multiple_of(jnp.where(top, N, 0), N), N)
    half_mine = jnp.where(top, 0, 1)
    load, send, recv_core, recv_x, recv_z, recv_gx, recv_gc, raw_send, raw_recv, mix_send, mix_recv, late_send, late_recv, wrap_send, wrap_recv, relay_send, relay_recv, keep = sems

    def place(z, x, core):
        return {"row": (z * 4 + x) * 2 + core}

    def peer(i):
        other = lax.rem(me + i, 8)
        return other, {"row": z * 8 + other}

    barrier = pltpu.get_barrier_semaphore()
    for i in range(1, 8):
        pl.semaphore_signal(barrier, inc=1, device_id=peer(i)[1], device_id_type=MESH)
    for i in range(1, 4):
        pl.semaphore_signal(barrier, inc=1, device_id=place(lax.rem(z + i, 4), x, core), device_id_type=MESH)
    for distance in (1, -1, 3, -3, 4, -4):
        pl.semaphore_signal(barrier, inc=1, device_id=pair(distance), device_id_type=MESH)

    partial_gram(x_ref, xb, part, load)
    pl.semaphore_wait(barrier, 16)

    h = 3 * N // 2
    q = h // 4
    mine = pl.ds(pl.multiple_of(core * h, 8), h)
    other = pl.ds(pl.multiple_of((1 - core) * h, 8), h)
    sent = []
    c = remote(part.at[other], in_core, send.at[0], recv_core, place(z, x, 1 - core))
    c.start()
    sent.append(c)

    size = EARLY // RAW_PARTS
    raw_f, raw_b = [], []
    for j in range(RAW_PARTS):
        at = pl.ds(j * size, size)
        raw_f.append(remote(xb.at[at], raw.at[0, at], raw_send.at[0, j], raw_recv.at[0, j], after))
        raw_b.append(remote(xb.at[at], raw.at[1, at], raw_send.at[1, j], raw_recv.at[1, j], before))

    def start_raw():
        for j in range(RAW_PARTS):
            pl.when(to_after)(raw_f[j].start)
            pl.when(to_before)(raw_b[j].start)

    if RAW_AT == 0:
        start_raw()
    c.wait_recv()
    half[...] = part[mine] + in_core[...]

    quarter = pl.ds(pl.multiple_of(x * q, 8), q)
    for i in range(1, 4):
        xt = lax.rem(x + i, 4)
        c = remote(half.at[pl.ds(pl.multiple_of(xt * q, 8), q)], in_x.at[x], send.at[i], recv_x.at[x], place(z, xt, core))
        c.start()
        sent.append(c)
    in_x[x] = half[quarter]
    for i in range(1, 4):
        xf = lax.rem(x + i, 4)
        remote(in_x.at[xf], in_x.at[xf], send.at[i], recv_x.at[xf], place(z, xf, core)).wait_recv()
    in_z[z] = (in_x[0] + in_x[1]) + (in_x[2] + in_x[3])

    for i in range(1, 4):
        zt = lax.rem(z + i, 4)
        c = remote(in_z.at[z], in_z.at[z], send.at[3 + i], recv_z.at[z], place(zt, x, core))
        c.start()
        sent.append(c)
    if RAW_AT == 1:
        start_raw()
    for i in range(1, 4):
        zf = lax.rem(z + i, 4)
        remote(in_z.at[zf], in_z.at[zf], send.at[3 + i], recv_z.at[zf], place(zf, x, core)).wait_recv()
    if RAW_AT == 2:
        start_raw()

    def rows_of(core, x):
        return total.at[pl.ds(pl.multiple_of(core * h + x * q, 8), q)]

    own = rows_of(core, x)
    own[...] = (in_z[0] + in_z[1]) + (in_z[2] + in_z[3])
    for i in range(1, 4):
        c = remote(own, own, send.at[6 + i], recv_gx.at[x], place(z, lax.rem(x + i, 4), core))
        c.start()
        sent.append(c)
    for i in range(4):
        xf = lax.rem(x + i, 4)
        there = rows_of(core, xf)
        if i:
            remote(there, there, send.at[6 + i], recv_gx.at[xf], place(z, xf, core)).wait_recv()
        c = remote(there, there, send.at[10 + i], recv_gc.at[xf], place(z, x, 1 - core))
        c.start()
        sent.append(c)
    for i in range(4):
        xf = lax.rem(x + i, 4)
        there = rows_of(1 - core, xf)
        remote(there, there, send.at[10 + i], recv_gc.at[xf], place(z, x, 1 - core)).wait_recv()
    for c in sent:
        c.wait_send()

    rounds(total, mix, *round_refs)

    seat = lax.rem(me, 8)
    share = N // 8

    def eighth(i):
        return pl.ds(pl.multiple_of(i * share, 8), share)

    first = jnp.where(k == 0, N, 0)
    mix_f = remote(
        mix.at[pl.ds(pl.multiple_of(first + seat * share, 8), share)], near.at[0, eighth(seat)],
        mix_send.at[0, 0], mix_recv.at[0, seat], after,
    )
    mix_b = remote(
        mix.at[pl.ds(pl.multiple_of(N + seat * share, 8), share)], near.at[1, eighth(seat)],
        mix_send.at[1, 0], mix_recv.at[1, seat], before,
    )
    pl.when(to_after)(mix_f.start)
    pl.when(to_before)(mix_b.start)

    def chunk(c):
        return pl.ds(c * CHUNK, CHUNK)

    def late_f(c):
        src = y.at[jnp.where(k == 0, 1, 0), chunk(c)]
        return remote(src, out_ref.at[chunk(c), pl.ds(0, N)], late_send.at[0, c], late_recv.at[0, c], after)

    def late_b(c):
        return remote(y.at[1, chunk(c)], out_ref.at[chunk(c), pl.ds(N, N)], late_send.at[1, c], late_recv.at[1, c], before)

    def rows_at(c, i):
        return pl.ds(c * CHUNK + i * QUARTER, QUARTER)

    def wrap_direct(c, i):
        at = rows_at(c, i)
        return remote(y.at[half_mine, at], out_ref.at[at, column_mine], wrap_send.at[c, i], wrap_recv.at[c, i], pair(step))

    def wrap_aside(c, i):
        at = rows_at(c, i)
        return remote(y.at[half_mine, at], relay.at[c, i - 1], wrap_send.at[c, i], relay_recv.at[c, i], pair(4 * step))

    def wrap_passed(c, i):
        dst = out_ref.at[rows_at(c, i), column_mine]
        return remote(relay.at[c, i - 1], dst, relay_send.at[c, i], wrap_recv.at[c, i], pair(-3 * step))

    def wrap_here(c, i):
        dst = out_ref.at[rows_at(c, i), column_here]
        return remote(y.at[half_mine, rows_at(c, i)], dst, wrap_send.at[c, i], wrap_recv.at[c, i], pair(step))

    def rotate(c):
        moved = mixed(xb[chunk(c), :], mix[...])
        y[0, chunk(c)] = moved[:, :N]
        y[1, chunk(c)] = moved[:, N:]

    def send_wraps(c):
        for i in range(4):
            if i:
                pl.when(wraps & (i >= direct_mine))(wrap_aside(c, i).start)
            if i < 3:
                pl.when(wraps & (i < direct_mine))(wrap_direct(c, i).start)

    for c in ORDER:
        if c * CHUNK >= EARLY:
            rotate(c)
            send_wraps(c)
            pl.when(to_after)(late_f(c).start)
            pl.when(to_before)(late_b(c).start)
        else:

            @pl.when(edge)
            def _():
                rotate(c)
                send_wraps(c)

    keep_left = pltpu.make_async_copy(y.at[0], out_ref.at[:, pl.ds(0, N)], keep.at[0])
    keep_right = pltpu.make_async_copy(y.at[0], out_ref.at[:, pl.ds(N, N)], keep.at[1])
    pl.when(k == 0)(keep_left.start)
    pl.when(k == last)(keep_right.start)

    def pass_on(c):
        for i in range(1, 4):

            @pl.when(edge & (i >= direct_passed))
            def _():
                wrap_aside(c, i).wait_recv()
                wrap_passed(c, i).start()

    def spread(which, first):
        first.wait_recv()
        for i in range(1, 8):
            slot = near.at[which, eighth(seat)]
            remote(slot, slot, mix_send.at[which, i], mix_recv.at[which, seat], peer(i)[1]).start()

    def early(which):
        return pltpu.make_async_copy(
            raw_y.at[which], out_ref.at[pl.ds(0, EARLY), pl.ds(which * N, N)], keep.at[which]
        )

    def finish(which, copies):
        for c in copies:
            c.wait_recv()
        for i in range(1, 8):
            there, device = peer(i)
            slot = near.at[which, eighth(there)]
            remote(slot, slot, mix_send.at[which, i], mix_recv.at[which, there], device).wait_recv()
        for c in range(EARLY // CHUNK):
            raw_y[which, chunk(c)] = mixed(raw[which, chunk(c)], near[which])
        early(which).start()

    pl.when(to_before)(lambda: spread(0, mix_f))
    pl.when(to_after)(lambda: spread(1, mix_b))
    for c in ORDER[:4]:
        pass_on(c)
    pl.when(to_before)(lambda: finish(0, raw_f))
    pl.when(to_after)(lambda: finish(1, raw_b))
    for c in ORDER[4:]:
        pass_on(c)

    def sent_mix(which):
        for i in range(1, 8):
            slot = near.at[which, eighth(seat)]
            remote(slot, slot, mix_send.at[which, i], mix_recv.at[which, seat], peer(i)[1]).wait_send()

    late = [c for c in ORDER if c * CHUNK >= EARLY]

    @pl.when(to_after)
    def _():
        for c in [mix_f] + raw_f + [late_f(c) for c in late]:
            c.wait_send()
        for c in late:
            late_b(c).wait_recv()
        sent_mix(1)
        early(1).wait()

    @pl.when(to_before)
    def _():
        for c in [mix_b] + raw_b + [late_b(c) for c in late]:
            c.wait_send()
        for c in late:
            late_f(c).wait_recv()
        sent_mix(0)
        early(0).wait()

    for c in ORDER:
        for i in range(4):

            @pl.when(wraps)
            def _():
                wrap_here(c, i).wait_send()
                wrap_here(c, i).wait_recv()

            if i:
                pl.when(edge & (i >= direct_passed))(wrap_passed(c, i).wait_send)
    pl.when(k == 0)(keep_left.wait)
    pl.when(k == last)(keep_right.wait)


def per_device(matrix):
    rows = matrix.shape[0]
    q = 3 * N // 8
    dma = pltpu.SemaphoreType.DMA
    f32 = jnp.float32
    return pl.pallas_call(
        step_kernel,
        out_shape=jax.ShapeDtypeStruct(matrix.shape, f32),
        in_specs=[pl.BlockSpec(memory_space=pl.ANY)],
        out_specs=pl.BlockSpec(memory_space=pl.ANY),
        scratch_shapes=[
            pltpu.VMEM((rows, 2 * N), f32),
            pltpu.VMEM((2, rows, N), f32),
            pltpu.VMEM((2, EARLY, 2 * N), f32),
            pltpu.VMEM((2, EARLY, N), f32),
            pltpu.VMEM((CHUNKS, 3, QUARTER, N), f32),
            pltpu.VMEM((3 * N, N), f32),
            pltpu.VMEM((4 * q, N), f32),
            pltpu.VMEM((3 * N, N), f32),
            pltpu.VMEM((4 * q, N), f32),
            pltpu.VMEM((4, q, N), f32),
            pltpu.VMEM((4, q, N), f32),
            pltpu.VMEM((2 * N, 2 * N), f32),
            pltpu.VMEM((2, N, 2 * N), f32),
            ROUND_SCRATCH,
            [
                dma((LOADS,)),
                dma((14,)),
                dma,
                dma((4,)),
                dma((4,)),
                dma((4,)),
                dma((4,)),
                dma((2, RAW_PARTS)),
                dma((2, RAW_PARTS)),
                dma((2, 8)),
                dma((2, 8)),
                dma((2, CHUNKS)),
                dma((2, CHUNKS)),
                dma((CHUNKS, 4)),
                dma((CHUNKS, 4)),
                dma((CHUNKS, 4)),
                dma((CHUNKS, 4)),
                dma((2,)),
            ],
        ],
        compiler_params=pltpu.CompilerParams(collective_id=0, has_side_effects=True, vmem_limit_bytes=48 << 20),
        name="jacobi_step",
    )(matrix)


def solution(mesh):
    return jax.shard_map(
        per_device, mesh=mesh, in_specs=(P("row", "pair"),), out_specs=P("row", "pair"), check_vma=False
    )
```

```python
import functools

import jax
import jax.numpy as jnp
from jax import lax
from jax.experimental import pallas as pl
from jax.experimental.pallas import tpu as pltpu
from jax.sharding import PartitionSpec as P

N = 128
D = 72
STAGES = 8
UNROLL = 8
MESH = pl.DeviceIdType.MESH
HIGH = lax.Precision.HIGHEST


def angles(a, b, g):
    d = b - a
    x = jnp.abs(d)
    y = 2.0 * g
    scale = jnp.where(jnp.maximum(x, jnp.abs(y)) < 2.0**-50, 2.0**80, 1.0)
    x = x * scale
    y = jnp.where(d < 0, -y, y) * scale
    turns = x > 0
    x = jnp.where(turns, x, 1.0)
    y = jnp.where(turns, y, 0.0)
    inv = lax.rsqrt(x * x + y * y)
    c2 = 0.5 + (0.5 * x) * inv
    inv_c = lax.rsqrt(c2)
    return c2 * inv_c, ((0.5 * y) * inv) * inv_c


def fan(x):
    return pltpu.roll(x, 0, 1, stride=1, stride_axis=0)


def fan_back(x):
    row = lax.broadcasted_iota(jnp.int32, x.shape, 0)
    for bit in (1, 2, 4):
        x = jnp.where((row & bit) != 0, pltpu.roll(x, N - bit, 1), x)
    parts = [x[m : m + 8] if m == 0 else pltpu.roll(x[m : m + 8], N - m, 1) for m in range(0, N, 8)]
    return jnp.concatenate(parts, axis=0)


def skew(transposed):
    return fan(fan_back(transposed).T)


def rounds(gram_ref, out_ref, a_ref, b_ref, g_ref, t_ref, ml_ref, mr_ref):
    cross = gram_ref[:, 0:16, :].reshape(N, N)
    packed = gram_ref[:, 16:32, :].reshape(N, N)
    row = lax.broadcasted_iota(jnp.int32, (N, N), 0)
    column = lax.broadcasted_iota(jnp.int32, (N, N), 1)
    flipped = packed.T
    right = jnp.where(row > column, packed, flipped)
    a_ref[...] = skew(jnp.where(row <= column, packed, flipped))[:D]
    b_ref[...] = skew(jnp.where(row == column, gram_ref[0, 32:33, :], right))[:D]
    g_ref[pl.ds(N, D), :] = skew(cross.T)[:D]
    t_ref[pl.ds(0, D), :] = skew(cross)[:D]
    ml_ref[...] = jnp.zeros_like(ml_ref)
    mr_ref[...] = jnp.zeros_like(mr_ref)
    ml_ref[0, pl.ds(0, 1), :] = jnp.ones((1, N), jnp.float32)
    mr_ref[1, pl.ds(N, 1), :] = jnp.ones((1, N), jnp.float32)

    def back(x, lanes):
        return pltpu.roll(x, N - lanes, 1)

    def one_round(rows, r, carry):
        da, db, dg, ea, eb, eg, a1, t1, g1, b1 = carry
        c, s = angles(da, db, dg)
        ce, se = back(c, 1), back(s, 1)
        na = c * (c * da - s * dg) - s * (c * dg - s * db)
        nb = se * (se * ea + ce * eg) + ce * (se * eg + ce * eb)
        ng = c * (se * a1 + ce * t1) - s * (se * g1 + ce * b1)
        n = max(rows, D)
        cd = fan(jnp.broadcast_to(c, (n, N)))
        sd = fan(jnp.broadcast_to(s, (n, N)))
        a, b = a_ref[...], b_ref[...]
        gw, tw = pl.ds(N - r, D), pl.ds(r, D)
        g, t = g_ref[gw, :], t_ref[tw, :]
        a, t = c * a - s * t, s * a + c * t
        g, b = c * g - s * b, s * g + c * b
        ch, sh = cd[:D], sd[:D]
        a, g = ch * a - sh * g, sh * a + ch * g
        t, b = ch * t - sh * b, sh * t + ch * b
        ahead = (back(na, 1), back(nb, 1), back(ng, 1), back(a[1:2], 1), back(t[2:3], 2), back(g[0:1], 1), back(b[1:2], 2))
        b = back(b, 1)
        t = back(t, 1)
        a_ref[...] = a
        b_ref[...] = b
        g_ref[gw, :] = g
        t_ref[tw, :] = t
        g_ref[pl.ds(N - 1 - r, 1), :] = t[1:2]
        t_ref[pl.ds(r + D, 1), :] = back(g[N - D : N - D + 1], N - D + 1)
        mw = pl.ds(N - r, rows)
        cm, sm = cd[:rows], sd[:rows]
        for h in range(2):
            left, right = ml_ref[h, pl.ds(0, rows), :], mr_ref[h, mw, :]
            ml_ref[h, pl.ds(0, rows), :] = cm * left - sm * right
            mr_ref[h, mw, :] = sm * left + cm * right
        return (na, nb, ng) + ahead

    def group(rows, i, carry):
        for u in range(UNROLL):
            carry = one_round(rows, UNROLL * i + u, carry)
        return carry

    first = (a_ref[0:1, :], b_ref[0:1, :], t_ref[0:1, :])
    carry = first + tuple(back(v, 1) for v in first + (a_ref[1:2, :], t_ref[1:2, :], g_ref[N + 1 : N + 2, :], b_ref[1:2, :]))
    for stage in range(STAGES):
        begin, end = N * stage // STAGES, N * (stage + 1) // STAGES
        carry = lax.fori_loop(begin // UNROLL, end // UNROLL, functools.partial(group, end), carry)
    for h in range(2):
        mr_ref[h, pl.ds(0, 1), :] = mr_ref[h, pl.ds(N, 1), :]
        out_ref[0:N, h * N : (h + 1) * N] = fan(fan_back(ml_ref[h]).T)
        out_ref[N:, h * N : (h + 1) * N] = fan(fan_back(mr_ref[h, 0:N, :]).T)


ROUND_SCRATCH = [
    pltpu.VMEM((D, N), jnp.float32),
    pltpu.VMEM((D, N), jnp.float32),
    pltpu.VMEM((208, N), jnp.float32),
    pltpu.VMEM((208, N), jnp.float32),
    pltpu.VMEM((2, N, N), jnp.float32),
    pltpu.VMEM((2, 2 * N, N), jnp.float32),
]


EARLY = 1024
RAW_PARTS = 8
RAW_FIRST = 2
CHUNK = 256
CHUNKS = 8
QUARTER = CHUNK // 4
ORDER = tuple(range(EARLY // CHUNK, CHUNKS)) + tuple(range(EARLY // CHUNK))
LOADS = 2


def remote(src, dst, send_sem, recv_sem, to):
    return pltpu.make_async_remote_copy(
        src_ref=src, dst_ref=dst, send_sem=send_sem, recv_sem=recv_sem, device_id=to, device_id_type=MESH
    )


def mixed(rows, mixing):
    return lax.dot_general(
        rows, mixing, (((1,), (1,)), ((), ())), precision=HIGH, preferred_element_type=jnp.float32
    )


def partial_gram(x_ref, xb, part, load):
    size = xb.shape[0] // LOADS
    copies = []
    for j in range(LOADS):
        at = pl.ds(j * size, size)
        copies.append(pltpu.make_async_copy(x_ref.at[at], xb.at[at], load.at[j]))
        copies[-1].start()

    def cross(u, v):
        return lax.dot_general(u, v, (((0,), (0,)), ((), ())), preferred_element_type=jnp.float32)

    even = odd = 0.0
    for j in range(LOADS):
        copies[j].wait()
        x = xb[pl.ds(j * size, size), :]
        high = x.astype(jnp.bfloat16)
        rest = x - high.astype(jnp.float32)
        mid = rest.astype(jnp.bfloat16)
        low = (rest - mid.astype(jnp.float32)).astype(jnp.bfloat16)
        even = even + (cross(high, high) + cross(mid, mid))
        odd = odd + (cross(high, mid) + cross(high, low))
    gram = even + (odd + odd.T)
    row = lax.broadcasted_iota(jnp.int32, (N, N), 0)
    column = lax.broadcasted_iota(jnp.int32, (N, N), 1)
    packed = jnp.where(row <= column, gram[:N, :N], gram[N:, N:])
    diagonal = jnp.sum(jnp.where(row == column, gram[N:, N:], 0.0), axis=0, keepdims=True)
    for e in range(8):
        part[e, 0:16] = gram[16 * e : 16 * e + 16, N:]
        part[e, 16:32] = packed[16 * e : 16 * e + 16]
        part[e, 32:33] = diagonal if e == 0 else jnp.zeros_like(diagonal)


def step_kernel(x_ref, out_ref, xb, y, raw, raw_y, relay, part, half, total, in_core, in_x, in_z, mix, near, round_refs, sems):
    me, k = lax.axis_index("row"), lax.axis_index("pair")
    core, x, z = lax.rem(me, 2), lax.rem(me // 2, 4), me // 8
    last = lax.axis_size("pair") - 1
    py, pz = k // 4, lax.rem(k, 4)
    to_after, to_before = pz < 3, pz > 0

    def pair(distance):
        return {"pair": lax.rem(k + distance + last + 1, last + 1)}

    after, before = pair(1), pair(-1)
    top = pz == 3
    edge = top | (pz == 0)
    wraps = (top & (py < 3)) | ((pz == 0) & (py > 0))
    step = jnp.where(top, 1, -1)
    direct_mine = jnp.where(top, 3 - py, py)
    direct_passed = jnp.where(top, 4 - py, py + 1)
    column_mine = pl.ds(pl.multiple_of(jnp.where(top, 0, N), N), N)
    column_here = pl.ds(pl.multiple_of(jnp.where(top, N, 0), N), N)
    half_mine = jnp.where(top, 0, 1)
    load, send, recv_core, recv_x, recv_z, recv_gx, recv_gc, raw_send, raw_recv, mix_send, mix_recv, late_send, late_recv, wrap_send, wrap_recv, relay_send, relay_recv, keep, near_ready, far_ready = sems

    def place(z, x, core):
        return {"row": (z * 4 + x) * 2 + core}

    def peer(i):
        other = lax.rem(me + i, 8)
        return other, {"row": z * 8 + other}

    barrier = pltpu.get_barrier_semaphore()

    def chip(distance, core):
        return {"pair": lax.rem(k + distance + last + 1, last + 1), "row": (z * 4 + x) * 2 + core}

    def exists(distance):
        return (k + distance >= 0) & (k + distance <= last)

    pairs = [
        (1, exists(1)), (-1, exists(-1)), (4, edge & exists(4)), (-4, edge & exists(-4)), (3, pz == 0), (-3, top),
    ]
    hears = 7
    for distance, there in pairs:
        hears = hears + 2 * there.astype(jnp.int32)

    def call(to):
        pl.semaphore_signal(barrier, inc=1, device_id=to, device_id_type=MESH)

    pl.when(core == 1)(lambda: call(place(z, x, 0)))
    for i in range(1, 4):
        call(place(lax.rem(z + i, 4), x, 1))
    for i in range(1, 4):
        call(place(z, lax.rem(x + i, 4), 0))
    for distance, there in pairs:
        pl.when(there)(lambda: call(chip(distance, 0)))

    partial_gram(x_ref, xb, part, load)

    @pl.when(core == 0)
    def _():
        pl.semaphore_wait(barrier, hears)
        pl.semaphore_signal(near_ready, inc=1, device_id=place(z, x, 1), device_id_type=MESH)

    pl.when(core == 1)(lambda: pl.semaphore_wait(near_ready, 1))

    mine = pl.ds(core * 4, 4)
    other = pl.ds((1 - core) * 4, 4)
    sent = []
    c = remote(part.at[other], in_core, send.at[0], recv_core, place(z, x, 1 - core))
    c.start()
    sent.append(c)

    size = EARLY // RAW_PARTS
    raw_f, raw_b = [], []
    for j in range(RAW_PARTS):
        at = pl.ds(j * size, size)
        raw_f.append(remote(xb.at[at], raw.at[0, at], raw_send.at[0, j], raw_recv.at[0, j], after))
        raw_b.append(remote(xb.at[at], raw.at[1, at], raw_send.at[1, j], raw_recv.at[1, j], before))

    def start_raw(begin, end):
        for j in range(begin, end):
            pl.when(to_after)(raw_f[j].start)
            pl.when(to_before)(raw_b[j].start)

    start_raw(0, RAW_FIRST)
    c.wait_recv()
    half[...] = part[mine] + in_core[...]

    for i in range(1, 4):
        xt = lax.rem(x + i, 4)
        c = remote(half.at[xt], in_x.at[x], send.at[i], recv_x.at[x], place(z, xt, core))
        c.start()
        sent.append(c)
    in_x[x] = half[x]
    for i in range(1, 4):
        xf = lax.rem(x + i, 4)
        remote(in_x.at[xf], in_x.at[xf], send.at[i], recv_x.at[xf], place(z, xf, core)).wait_recv()
    in_z[z] = (in_x[0] + in_x[1]) + (in_x[2] + in_x[3])

    @pl.when(core == 1)
    def _():
        pl.semaphore_wait(barrier, 6)
        pl.semaphore_signal(far_ready, inc=1, device_id=place(z, x, 0), device_id_type=MESH)

    pl.when(core == 0)(lambda: pl.semaphore_wait(far_ready, 1))
    for i in range(1, 4):
        zt = lax.rem(z + i, 4)
        c = remote(in_z.at[z], in_z.at[z], send.at[3 + i], recv_z.at[z], place(zt, x, core))
        c.start()
        sent.append(c)
    for i in range(1, 4):
        zf = lax.rem(z + i, 4)
        remote(in_z.at[zf], in_z.at[zf], send.at[3 + i], recv_z.at[zf], place(zf, x, core)).wait_recv()
    start_raw(RAW_FIRST, RAW_PARTS)

    def rows_of(core, x):
        return total.at[core * 4 + x]

    own = rows_of(core, x)
    own[...] = (in_z[0] + in_z[1]) + (in_z[2] + in_z[3])
    for i in range(1, 4):
        c = remote(own, own, send.at[6 + i], recv_gx.at[x], place(z, lax.rem(x + i, 4), core))
        c.start()
        sent.append(c)
    for i in range(4):
        xf = lax.rem(x + i, 4)
        there = rows_of(core, xf)
        if i:
            remote(there, there, send.at[6 + i], recv_gx.at[xf], place(z, xf, core)).wait_recv()
        c = remote(there, there, send.at[10 + i], recv_gc.at[xf], place(z, x, 1 - core))
        c.start()
        sent.append(c)
    for i in range(4):
        xf = lax.rem(x + i, 4)
        there = rows_of(1 - core, xf)
        remote(there, there, send.at[10 + i], recv_gc.at[xf], place(z, x, 1 - core)).wait_recv()
    for c in sent:
        c.wait_send()

    rounds(total, mix, *round_refs)

    seat = lax.rem(me, 8)
    share = N // 8

    def eighth(i):
        return pl.ds(pl.multiple_of(i * share, 8), share)

    first = jnp.where(k == 0, N, 0)
    mix_f = remote(
        mix.at[pl.ds(pl.multiple_of(first + seat * share, 8), share)], near.at[0, eighth(seat)],
        mix_send.at[0, 0], mix_recv.at[0, seat], after,
    )
    mix_b = remote(
        mix.at[pl.ds(pl.multiple_of(N + seat * share, 8), share)], near.at[1, eighth(seat)],
        mix_send.at[1, 0], mix_recv.at[1, seat], before,
    )
    pl.when(to_after)(mix_f.start)
    pl.when(to_before)(mix_b.start)

    def chunk(c):
        return pl.ds(c * CHUNK, CHUNK)

    def late_f(c):
        src = y.at[jnp.where(k == 0, 1, 0), chunk(c)]
        return remote(src, out_ref.at[chunk(c), pl.ds(0, N)], late_send.at[0, c], late_recv.at[0, c], after)

    def late_b(c):
        return remote(y.at[1, chunk(c)], out_ref.at[chunk(c), pl.ds(N, N)], late_send.at[1, c], late_recv.at[1, c], before)

    def rows_at(c, i):
        return pl.ds(c * CHUNK + i * QUARTER, QUARTER)

    def wrap_direct(c, i):
        at = rows_at(c, i)
        return remote(y.at[half_mine, at], out_ref.at[at, column_mine], wrap_send.at[c, i], wrap_recv.at[c, i], pair(step))

    def wrap_aside(c, i):
        at = rows_at(c, i)
        return remote(y.at[half_mine, at], relay.at[c, i - 1], wrap_send.at[c, i], relay_recv.at[c, i], pair(4 * step))

    def wrap_passed(c, i):
        dst = out_ref.at[rows_at(c, i), column_mine]
        return remote(relay.at[c, i - 1], dst, relay_send.at[c, i], wrap_recv.at[c, i], pair(-3 * step))

    def wrap_here(c, i):
        dst = out_ref.at[rows_at(c, i), column_here]
        return remote(y.at[half_mine, rows_at(c, i)], dst, wrap_send.at[c, i], wrap_recv.at[c, i], pair(step))

    def rotate(c):
        moved = mixed(xb[chunk(c), :], mix[...])
        y[0, chunk(c)] = moved[:, :N]
        y[1, chunk(c)] = moved[:, N:]

    def send_wraps(c):
        for i in range(4):
            if i:
                pl.when(wraps & (i >= direct_mine))(wrap_aside(c, i).start)
            if i < 3:
                pl.when(wraps & (i < direct_mine))(wrap_direct(c, i).start)

    for c in ORDER:
        if c * CHUNK >= EARLY:
            rotate(c)
            send_wraps(c)
            pl.when(to_after)(late_f(c).start)
            pl.when(to_before)(late_b(c).start)
        else:

            @pl.when(edge)
            def _():
                rotate(c)
                send_wraps(c)

    keep_left = pltpu.make_async_copy(y.at[0], out_ref.at[:, pl.ds(0, N)], keep.at[0])
    keep_right = pltpu.make_async_copy(y.at[0], out_ref.at[:, pl.ds(N, N)], keep.at[1])
    pl.when(k == 0)(keep_left.start)
    pl.when(k == last)(keep_right.start)

    def pass_on(c):
        for i in range(1, 4):

            @pl.when(edge & (i >= direct_passed))
            def _():
                wrap_aside(c, i).wait_recv()
                wrap_passed(c, i).start()

    def spread(which, first):
        first.wait_recv()
        for i in range(1, 8):
            slot = near.at[which, eighth(seat)]
            remote(slot, slot, mix_send.at[which, i], mix_recv.at[which, seat], peer(i)[1]).start()

    def early(which):
        return pltpu.make_async_copy(
            raw_y.at[which], out_ref.at[pl.ds(0, EARLY), pl.ds(which * N, N)], keep.at[which]
        )

    def finish(which, copies):
        for c in copies:
            c.wait_recv()
        for i in range(1, 8):
            there, device = peer(i)
            slot = near.at[which, eighth(there)]
            remote(slot, slot, mix_send.at[which, i], mix_recv.at[which, there], device).wait_recv()
        for c in range(EARLY // CHUNK):
            raw_y[which, chunk(c)] = mixed(raw[which, chunk(c)], near[which])
        early(which).start()

    pl.when(to_before)(lambda: spread(0, mix_f))
    pl.when(to_after)(lambda: spread(1, mix_b))
    for c in ORDER[:4]:
        pass_on(c)
    pl.when(to_before)(lambda: finish(0, raw_f))
    pl.when(to_after)(lambda: finish(1, raw_b))
    for c in ORDER[4:]:
        pass_on(c)

    def sent_mix(which):
        for i in range(1, 8):
            slot = near.at[which, eighth(seat)]
            remote(slot, slot, mix_send.at[which, i], mix_recv.at[which, seat], peer(i)[1]).wait_send()

    late = [c for c in ORDER if c * CHUNK >= EARLY]

    @pl.when(to_after)
    def _():
        for c in [mix_f] + raw_f + [late_f(c) for c in late]:
            c.wait_send()
        for c in late:
            late_b(c).wait_recv()
        sent_mix(1)
        early(1).wait()

    @pl.when(to_before)
    def _():
        for c in [mix_b] + raw_b + [late_b(c) for c in late]:
            c.wait_send()
        for c in late:
            late_f(c).wait_recv()
        sent_mix(0)
        early(0).wait()

    for c in ORDER:
        for i in range(4):

            @pl.when(wraps)
            def _():
                wrap_here(c, i).wait_send()
                wrap_here(c, i).wait_recv()

            if i:
                pl.when(edge & (i >= direct_passed))(wrap_passed(c, i).wait_send)
    pl.when(k == 0)(keep_left.wait)
    pl.when(k == last)(keep_right.wait)


def per_device(matrix):
    rows = matrix.shape[0]
    eighth = (33, N)
    dma = pltpu.SemaphoreType.DMA
    f32 = jnp.float32
    return pl.pallas_call(
        step_kernel,
        out_shape=jax.ShapeDtypeStruct(matrix.shape, f32),
        in_specs=[pl.BlockSpec(memory_space=pltpu.HBM)],
        out_specs=pl.BlockSpec(memory_space=pl.ANY),
        scratch_shapes=[
            pltpu.VMEM((rows, 2 * N), f32),
            pltpu.VMEM((2, rows, N), f32),
            pltpu.VMEM((2, EARLY, 2 * N), f32),
            pltpu.VMEM((2, EARLY, N), f32),
            pltpu.VMEM((CHUNKS, 3, QUARTER, N), f32),
            pltpu.VMEM((8, *eighth), f32),
            pltpu.VMEM((4, *eighth), f32),
            pltpu.VMEM((8, *eighth), f32),
            pltpu.VMEM((4, *eighth), f32),
            pltpu.VMEM((4, *eighth), f32),
            pltpu.VMEM((4, *eighth), f32),
            pltpu.VMEM((2 * N, 2 * N), f32),
            pltpu.VMEM((2, N, 2 * N), f32),
            ROUND_SCRATCH,
            [
                dma((LOADS,)),
                dma((14,)),
                dma,
                dma((4,)),
                dma((4,)),
                dma((4,)),
                dma((4,)),
                dma((2, RAW_PARTS)),
                dma((2, RAW_PARTS)),
                dma((2, 8)),
                dma((2, 8)),
                dma((2, CHUNKS)),
                dma((2, CHUNKS)),
                dma((CHUNKS, 4)),
                dma((CHUNKS, 4)),
                dma((CHUNKS, 4)),
                dma((CHUNKS, 4)),
                dma((2,)),
                pltpu.SemaphoreType.REGULAR,
                pltpu.SemaphoreType.REGULAR,
            ],
        ],
        compiler_params=pltpu.CompilerParams(collective_id=0, has_side_effects=True, vmem_limit_bytes=48 << 20),
        name="jacobi_step",
    )(matrix)


def solution(mesh):
    return jax.shard_map(
        per_device, mesh=mesh, in_specs=(P("row", "pair"),), out_specs=P("row", "pair"), check_vma=False
    )
```

```python
import functools

import jax
import jax.numpy as jnp
from jax import lax
from jax.experimental import pallas as pl
from jax.experimental.pallas import tpu as pltpu
from jax.sharding import PartitionSpec as P

N = 128
D = 72
STAGES = 4
UNROLL = 16
MESH = pl.DeviceIdType.MESH
HIGH = lax.Precision.HIGHEST


def angles(a, b, g):
    d = b - a
    x = jnp.abs(d)
    y = 2.0 * g
    scale = jnp.where(jnp.maximum(x, jnp.abs(y)) < 2.0**-50, 2.0**80, 1.0)
    x = x * scale
    y = jnp.where(d < 0, -y, y) * scale
    turns = x > 0
    x = jnp.where(turns, x, 1.0)
    y = jnp.where(turns, y, 0.0)
    inv = lax.rsqrt(x * x + y * y)
    c2 = 0.5 + (0.5 * x) * inv
    inv_c = lax.rsqrt(c2)
    return c2 * inv_c, ((0.5 * y) * inv) * inv_c


def fan(x):
    return pltpu.roll(x, 0, 1, stride=1, stride_axis=0)


def fan_back(x):
    row = lax.broadcasted_iota(jnp.int32, x.shape, 0)
    for bit in (1, 2, 4):
        x = jnp.where((row & bit) != 0, pltpu.roll(x, N - bit, 1), x)
    parts = [x[m : m + 8] if m == 0 else pltpu.roll(x[m : m + 8], N - m, 1) for m in range(0, N, 8)]
    return jnp.concatenate(parts, axis=0)


def skew(transposed):
    return fan(fan_back(transposed).T)


def rounds(gram_ref, out_ref, a_ref, b_ref, g_ref, t_ref, ml_ref, mr_ref):
    cross = gram_ref[:, 0:16, :].reshape(N, N)
    packed = gram_ref[:, 16:32, :].reshape(N, N)
    row = lax.broadcasted_iota(jnp.int32, (N, N), 0)
    column = lax.broadcasted_iota(jnp.int32, (N, N), 1)
    flipped = packed.T
    right = jnp.where(row > column, packed, flipped)
    a_ref[...] = skew(jnp.where(row <= column, packed, flipped))[:D]
    b_ref[...] = skew(jnp.where(row == column, gram_ref[0, 32:33, :], right))[:D]
    g_ref[pl.ds(N, D), :] = skew(cross.T)[:D]
    t_ref[pl.ds(0, D), :] = skew(cross)[:D]
    ml_ref[...] = jnp.zeros_like(ml_ref)
    mr_ref[...] = jnp.zeros_like(mr_ref)
    ml_ref[0, pl.ds(0, 1), :] = jnp.ones((1, N), jnp.float32)
    mr_ref[1, pl.ds(N, 1), :] = jnp.ones((1, N), jnp.float32)

    def back(x, lanes):
        return pltpu.roll(x, N - lanes, 1)

    def turned(a, t, g, b, c, s, cc, ss):
        a, t = c * a - s * t, s * a + c * t
        g, b = c * g - s * b, s * g + c * b
        a, g = cc * a - ss * g, ss * a + cc * g
        t, b = cc * t - ss * b, ss * t + cc * b
        return a, t, g, b

    def full_round(rows, r, c, s):
        n = max(rows, D)
        cd = fan(jnp.broadcast_to(c, (n, N)))
        sd = fan(jnp.broadcast_to(s, (n, N)))
        gw, tw = pl.ds(N - r, D), pl.ds(r, D)
        a, t, g, b = turned(a_ref[...], t_ref[tw, :], g_ref[gw, :], b_ref[...], c, s, cd[:D], sd[:D])
        b_next, t_next = back(b, 1), back(t, 1)
        a_ref[...] = a
        b_ref[...] = b_next
        g_ref[gw, :] = g
        t_ref[tw, :] = t_next
        g_ref[pl.ds(N - 1 - r, 1), :] = t_next[1:2]
        t_ref[pl.ds(r + D, 1), :] = back(g[N - D : N - D + 1], N - D + 1)
        mw = pl.ds(N - r, rows)
        cm, sm = cd[:rows], sd[:rows]
        for h in range(2):
            left, right = ml_ref[h, pl.ds(0, rows), :], mr_ref[h, mw, :]
            ml_ref[h, pl.ds(0, rows), :] = cm * left - sm * right
            mr_ref[h, mw, :] = sm * left + cm * right
        return a, t, g, b

    def two_rounds(rows, r, carry):
        (a0, b0, g0), (a1, b1, g1), (a2, b2, g2), near, middle, far = carry
        c0, s0 = angles(a0, b0, g0)
        c1, s1, c2, s2 = back(c0, 1), back(s0, 1), back(c0, 2), back(s0, 2)
        diag0 = turned(a0, g0, g0, b0, c0, s0, c0, s0)
        diag1 = turned(a1, g1, g1, b1, c1, s1, c1, s1)
        diag2 = turned(a2, g2, g2, b2, c2, s2, c2, s2)
        near = turned(*near, c1, s1, c0, s0)
        middle = turned(*middle, c2, s2, c1, s1)
        far = turned(*far, c2, s2, c0, s0)
        full_round(rows, r, c0, s0)
        cross = diag1[2]
        a0, b0, g0 = diag0[0], diag1[3], near[1]
        a1, b1, g1 = diag1[0], diag2[3], middle[1]
        c0, s0 = angles(a0, b0, g0)
        c1, s1 = angles(a1, b1, g1)
        diag0 = turned(a0, g0, g0, b0, c0, s0, c0, s0)
        diag1 = turned(a1, g1, g1, b1, c1, s1, c1, s1)
        near = turned(near[0], far[1], cross, middle[3], c1, s1, c0, s0)
        a, t, g, b = full_round(rows, r + 1, c0, s0)
        first = (diag0[0], diag1[3], near[1])
        return (
            first,
            tuple(back(v, 1) for v in first),
            tuple(back(v, 2) for v in first),
            (back(a[1:2], 1), back(t[2:3], 2), back(g[0:1], 1), back(b[1:2], 2)),
            (back(a[1:2], 2), back(t[2:3], 3), back(g[0:1], 2), back(b[1:2], 3)),
            (back(a[2:3], 2), back(t[3:4], 3), back(g[1:2], 2), back(b[2:3], 3)),
        )

    def group(rows, i, carry):
        for u in range(0, UNROLL, 2):
            carry = two_rounds(rows, UNROLL * i + u, carry)
        return carry

    def entries(d, lanes):
        rows = (a_ref[d : d + 1, :], t_ref[d : d + 1, :], g_ref[N + d : N + d + 1, :], b_ref[d : d + 1, :])
        return tuple(back(v, lanes) for v in rows)

    first = (a_ref[0:1, :], b_ref[0:1, :], t_ref[0:1, :])
    carry = (
        first, tuple(back(v, 1) for v in first), tuple(back(v, 2) for v in first), entries(1, 1), entries(1, 2), entries(2, 2)
    )
    for stage in range(STAGES):
        begin, end = N * stage // STAGES, N * (stage + 1) // STAGES
        carry = lax.fori_loop(begin // UNROLL, end // UNROLL, functools.partial(group, end), carry)
    for h in range(2):
        mr_ref[h, pl.ds(0, 1), :] = mr_ref[h, pl.ds(N, 1), :]
        out_ref[0:N, h * N : (h + 1) * N] = fan(fan_back(ml_ref[h]).T)
        out_ref[N:, h * N : (h + 1) * N] = fan(fan_back(mr_ref[h, 0:N, :]).T)


ROUND_SCRATCH = [
    pltpu.VMEM((D, N), jnp.float32),
    pltpu.VMEM((D, N), jnp.float32),
    pltpu.VMEM((208, N), jnp.float32),
    pltpu.VMEM((208, N), jnp.float32),
    pltpu.VMEM((2, N, N), jnp.float32),
    pltpu.VMEM((2, 2 * N, N), jnp.float32),
]


EARLY = 1024
RAW_PARTS = 8
RAW_FIRST = 0
CHUNK = 256
CHUNKS = 8
QUARTER = CHUNK // 4
ORDER = tuple(range(EARLY // CHUNK, CHUNKS)) + tuple(range(EARLY // CHUNK))
LOADS = 2


def remote(src, dst, send_sem, recv_sem, to):
    return pltpu.make_async_remote_copy(
        src_ref=src, dst_ref=dst, send_sem=send_sem, recv_sem=recv_sem, device_id=to, device_id_type=MESH
    )


def mixed(rows, mixing):
    return lax.dot_general(
        rows, mixing, (((1,), (1,)), ((), ())), precision=HIGH, preferred_element_type=jnp.float32
    )


def partial_gram(x_ref, xb, part, load):
    size = xb.shape[0] // LOADS
    copies = []
    for j in range(LOADS):
        at = pl.ds(j * size, size)
        copies.append(pltpu.make_async_copy(x_ref.at[at], xb.at[at], load.at[j]))
        copies[-1].start()

    def cross(u, v):
        return lax.dot_general(u, v, (((0,), (0,)), ((), ())), preferred_element_type=jnp.float32)

    even = odd = 0.0
    for j in range(LOADS):
        copies[j].wait()
        x = xb[pl.ds(j * size, size), :]
        high = x.astype(jnp.bfloat16)
        rest = x - high.astype(jnp.float32)
        mid = rest.astype(jnp.bfloat16)
        low = (rest - mid.astype(jnp.float32)).astype(jnp.bfloat16)
        even = even + (cross(high, high) + cross(mid, mid))
        odd = odd + (cross(high, mid) + cross(high, low))
    gram = even + (odd + odd.T)
    row = lax.broadcasted_iota(jnp.int32, (N, N), 0)
    column = lax.broadcasted_iota(jnp.int32, (N, N), 1)
    packed = jnp.where(row <= column, gram[:N, :N], gram[N:, N:])
    diagonal = jnp.sum(jnp.where(row == column, gram[N:, N:], 0.0), axis=0, keepdims=True)
    for e in range(8):
        part[e, 0:16] = gram[16 * e : 16 * e + 16, N:]
        part[e, 16:32] = packed[16 * e : 16 * e + 16]
        part[e, 32:33] = diagonal if e == 0 else jnp.zeros_like(diagonal)


def step_kernel(x_ref, out_ref, xb, y, raw, raw_y, relay, part, half, total, in_core, in_x, in_z, mix, near, round_refs, sems):
    me, k = lax.axis_index("row"), lax.axis_index("pair")
    core, x, z = lax.rem(me, 2), lax.rem(me // 2, 4), me // 8
    last = lax.axis_size("pair") - 1
    py, pz = k // 4, lax.rem(k, 4)
    to_after, to_before = pz < 3, pz > 0

    def pair(distance):
        return {"pair": lax.rem(k + distance + last + 1, last + 1)}

    after, before = pair(1), pair(-1)
    top = pz == 3
    edge = top | (pz == 0)
    wraps = (top & (py < 3)) | ((pz == 0) & (py > 0))
    step = jnp.where(top, 1, -1)
    direct_mine = jnp.where(top, 3 - py, py)
    direct_passed = jnp.where(top, 4 - py, py + 1)
    column_mine = pl.ds(pl.multiple_of(jnp.where(top, 0, N), N), N)
    column_here = pl.ds(pl.multiple_of(jnp.where(top, N, 0), N), N)
    half_mine = jnp.where(top, 0, 1)
    load, send, recv_core, recv_x, recv_z, recv_gx, recv_gc, raw_send, raw_recv, mix_send, mix_recv, late_send, late_recv, wrap_send, wrap_recv, relay_send, relay_recv, keep, near_ready, far_ready = sems

    def place(z, x, core):
        return {"row": (z * 4 + x) * 2 + core}

    def peer(i):
        other = lax.rem(me + i, 8)
        return other, {"row": z * 8 + other}

    barrier = pltpu.get_barrier_semaphore()

    def chip(distance, core):
        return {"pair": lax.rem(k + distance + last + 1, last + 1), "row": (z * 4 + x) * 2 + core}

    def exists(distance):
        return (k + distance >= 0) & (k + distance <= last)

    pairs = [
        (1, exists(1)), (-1, exists(-1)), (4, edge & exists(4)), (-4, edge & exists(-4)), (3, pz == 0), (-3, top),
    ]
    hears = 7
    for distance, there in pairs:
        hears = hears + 2 * there.astype(jnp.int32)

    def call(to):
        pl.semaphore_signal(barrier, inc=1, device_id=to, device_id_type=MESH)

    pl.when(core == 1)(lambda: call(place(z, x, 0)))
    for i in range(1, 4):
        call(place(lax.rem(z + i, 4), x, 1))
    for i in range(1, 4):
        call(place(z, lax.rem(x + i, 4), 0))
    for distance, there in pairs:
        pl.when(there)(lambda: call(chip(distance, 0)))

    partial_gram(x_ref, xb, part, load)

    @pl.when(core == 0)
    def _():
        pl.semaphore_wait(barrier, hears)
        pl.semaphore_signal(near_ready, inc=1, device_id=place(z, x, 1), device_id_type=MESH)

    pl.when(core == 1)(lambda: pl.semaphore_wait(near_ready, 1))

    mine = pl.ds(core * 4, 4)
    other = pl.ds((1 - core) * 4, 4)
    sent = []
    c = remote(part.at[other], in_core, send.at[0], recv_core, place(z, x, 1 - core))
    c.start()
    sent.append(c)

    size = EARLY // RAW_PARTS
    raw_f, raw_b = [], []
    for j in range(RAW_PARTS):
        at = pl.ds(j * size, size)
        raw_f.append(remote(xb.at[at], raw.at[0, at], raw_send.at[0, j], raw_recv.at[0, j], after))
        raw_b.append(remote(xb.at[at], raw.at[1, at], raw_send.at[1, j], raw_recv.at[1, j], before))

    def start_raw(begin, end):
        for j in range(begin, end):
            pl.when(to_after)(raw_f[j].start)
            pl.when(to_before)(raw_b[j].start)

    start_raw(0, RAW_FIRST)
    c.wait_recv()
    half[...] = part[mine] + in_core[...]

    for i in range(1, 4):
        xt = lax.rem(x + i, 4)
        c = remote(half.at[xt], in_x.at[x], send.at[i], recv_x.at[x], place(z, xt, core))
        c.start()
        sent.append(c)
    in_x[x] = half[x]
    for i in range(1, 4):
        xf = lax.rem(x + i, 4)
        remote(in_x.at[xf], in_x.at[xf], send.at[i], recv_x.at[xf], place(z, xf, core)).wait_recv()
    in_z[z] = (in_x[0] + in_x[1]) + (in_x[2] + in_x[3])

    @pl.when(core == 1)
    def _():
        pl.semaphore_wait(barrier, 6)
        pl.semaphore_signal(far_ready, inc=1, device_id=place(z, x, 0), device_id_type=MESH)

    pl.when(core == 0)(lambda: pl.semaphore_wait(far_ready, 1))
    for i in range(1, 4):
        zt = lax.rem(z + i, 4)
        c = remote(in_z.at[z], in_z.at[z], send.at[3 + i], recv_z.at[z], place(zt, x, core))
        c.start()
        sent.append(c)
    for i in range(1, 4):
        zf = lax.rem(z + i, 4)
        remote(in_z.at[zf], in_z.at[zf], send.at[3 + i], recv_z.at[zf], place(zf, x, core)).wait_recv()
    start_raw(RAW_FIRST, RAW_PARTS)

    def rows_of(core, x):
        return total.at[core * 4 + x]

    own = rows_of(core, x)
    own[...] = (in_z[0] + in_z[1]) + (in_z[2] + in_z[3])
    for i in range(1, 4):
        c = remote(own, own, send.at[6 + i], recv_gx.at[x], place(z, lax.rem(x + i, 4), core))
        c.start()
        sent.append(c)
    for i in range(4):
        xf = lax.rem(x + i, 4)
        there = rows_of(core, xf)
        if i:
            remote(there, there, send.at[6 + i], recv_gx.at[xf], place(z, xf, core)).wait_recv()
        c = remote(there, there, send.at[10 + i], recv_gc.at[xf], place(z, x, 1 - core))
        c.start()
        sent.append(c)
    for i in range(4):
        xf = lax.rem(x + i, 4)
        there = rows_of(1 - core, xf)
        remote(there, there, send.at[10 + i], recv_gc.at[xf], place(z, x, 1 - core)).wait_recv()
    for c in sent:
        c.wait_send()

    rounds(total, mix, *round_refs)

    seat = lax.rem(me, 8)
    share = N // 8

    def eighth(i):
        return pl.ds(pl.multiple_of(i * share, 8), share)

    first = jnp.where(k == 0, N, 0)
    mix_f = remote(
        mix.at[pl.ds(pl.multiple_of(first + seat * share, 8), share)], near.at[0, eighth(seat)],
        mix_send.at[0, 0], mix_recv.at[0, seat], after,
    )
    mix_b = remote(
        mix.at[pl.ds(pl.multiple_of(N + seat * share, 8), share)], near.at[1, eighth(seat)],
        mix_send.at[1, 0], mix_recv.at[1, seat], before,
    )
    pl.when(to_after)(mix_f.start)
    pl.when(to_before)(mix_b.start)

    def chunk(c):
        return pl.ds(c * CHUNK, CHUNK)

    def late_f(c):
        src = y.at[jnp.where(k == 0, 1, 0), chunk(c)]
        return remote(src, out_ref.at[chunk(c), pl.ds(0, N)], late_send.at[0, c], late_recv.at[0, c], after)

    def late_b(c):
        return remote(y.at[1, chunk(c)], out_ref.at[chunk(c), pl.ds(N, N)], late_send.at[1, c], late_recv.at[1, c], before)

    def rows_at(c, i):
        return pl.ds(c * CHUNK + i * QUARTER, QUARTER)

    def wrap_direct(c, i):
        at = rows_at(c, i)
        return remote(y.at[half_mine, at], out_ref.at[at, column_mine], wrap_send.at[c, i], wrap_recv.at[c, i], pair(step))

    def wrap_aside(c, i):
        at = rows_at(c, i)
        return remote(y.at[half_mine, at], relay.at[c, i - 1], wrap_send.at[c, i], relay_recv.at[c, i], pair(4 * step))

    def wrap_passed(c, i):
        dst = out_ref.at[rows_at(c, i), column_mine]
        return remote(relay.at[c, i - 1], dst, relay_send.at[c, i], wrap_recv.at[c, i], pair(-3 * step))

    def wrap_here(c, i):
        dst = out_ref.at[rows_at(c, i), column_here]
        return remote(y.at[half_mine, rows_at(c, i)], dst, wrap_send.at[c, i], wrap_recv.at[c, i], pair(step))

    def rotate(c):
        moved = mixed(xb[chunk(c), :], mix[...])
        y[0, chunk(c)] = moved[:, :N]
        y[1, chunk(c)] = moved[:, N:]

    def send_aside(c):
        for i in range(1, 4):
            pl.when(wraps & (i >= direct_mine))(wrap_aside(c, i).start)

    for c in ORDER:
        if c * CHUNK >= EARLY:
            rotate(c)
            send_aside(c)
            pl.when(to_after)(late_f(c).start)
            pl.when(to_before)(late_b(c).start)
        else:

            @pl.when(edge)
            def _():
                rotate(c)
                send_aside(c)

    for c in ORDER:
        for i in range(3):
            pl.when(wraps & (i < direct_mine))(wrap_direct(c, i).start)

    keep_left = pltpu.make_async_copy(y.at[0], out_ref.at[:, pl.ds(0, N)], keep.at[0])
    keep_right = pltpu.make_async_copy(y.at[0], out_ref.at[:, pl.ds(N, N)], keep.at[1])
    pl.when(k == 0)(keep_left.start)
    pl.when(k == last)(keep_right.start)

    def pass_on(c):
        for i in range(1, 4):

            @pl.when(edge & (i >= direct_passed))
            def _():
                wrap_aside(c, i).wait_recv()
                wrap_passed(c, i).start()

    def spread(which, first):
        first.wait_recv()
        for i in range(1, 8):
            slot = near.at[which, eighth(seat)]
            remote(slot, slot, mix_send.at[which, i], mix_recv.at[which, seat], peer(i)[1]).start()

    def early(which):
        return pltpu.make_async_copy(
            raw_y.at[which], out_ref.at[pl.ds(0, EARLY), pl.ds(which * N, N)], keep.at[which]
        )

    def finish(which, copies):
        for c in copies:
            c.wait_recv()
        for i in range(1, 8):
            there, device = peer(i)
            slot = near.at[which, eighth(there)]
            remote(slot, slot, mix_send.at[which, i], mix_recv.at[which, there], device).wait_recv()
        for c in range(EARLY // CHUNK):
            raw_y[which, chunk(c)] = mixed(raw[which, chunk(c)], near[which])
        early(which).start()

    pl.when(to_before)(lambda: spread(0, mix_f))
    pl.when(to_after)(lambda: spread(1, mix_b))
    for c in ORDER:
        pass_on(c)
    pl.when(to_before)(lambda: finish(0, raw_f))
    pl.when(to_after)(lambda: finish(1, raw_b))

    def sent_mix(which):
        for i in range(1, 8):
            slot = near.at[which, eighth(seat)]
            remote(slot, slot, mix_send.at[which, i], mix_recv.at[which, seat], peer(i)[1]).wait_send()

    late = [c for c in ORDER if c * CHUNK >= EARLY]

    @pl.when(to_after)
    def _():
        for c in [mix_f] + raw_f + [late_f(c) for c in late]:
            c.wait_send()
        for c in late:
            late_b(c).wait_recv()
        sent_mix(1)
        early(1).wait()

    @pl.when(to_before)
    def _():
        for c in [mix_b] + raw_b + [late_b(c) for c in late]:
            c.wait_send()
        for c in late:
            late_f(c).wait_recv()
        sent_mix(0)
        early(0).wait()

    for c in ORDER:
        for i in range(4):

            @pl.when(wraps)
            def _():
                wrap_here(c, i).wait_send()
                wrap_here(c, i).wait_recv()

            if i:
                pl.when(edge & (i >= direct_passed))(wrap_passed(c, i).wait_send)
    pl.when(k == 0)(keep_left.wait)
    pl.when(k == last)(keep_right.wait)


def per_device(matrix):
    rows = matrix.shape[0]
    eighth = (33, N)
    dma = pltpu.SemaphoreType.DMA
    f32 = jnp.float32
    return pl.pallas_call(
        step_kernel,
        out_shape=jax.ShapeDtypeStruct(matrix.shape, f32),
        in_specs=[pl.BlockSpec(memory_space=pltpu.HBM)],
        out_specs=pl.BlockSpec(memory_space=pl.ANY),
        scratch_shapes=[
            pltpu.VMEM((rows, 2 * N), f32),
            pltpu.VMEM((2, rows, N), f32),
            pltpu.VMEM((2, EARLY, 2 * N), f32),
            pltpu.VMEM((2, EARLY, N), f32),
            pltpu.VMEM((CHUNKS, 3, QUARTER, N), f32),
            pltpu.VMEM((8, *eighth), f32),
            pltpu.VMEM((4, *eighth), f32),
            pltpu.VMEM((8, *eighth), f32),
            pltpu.VMEM((4, *eighth), f32),
            pltpu.VMEM((4, *eighth), f32),
            pltpu.VMEM((4, *eighth), f32),
            pltpu.VMEM((2 * N, 2 * N), f32),
            pltpu.VMEM((2, N, 2 * N), f32),
            ROUND_SCRATCH,
            [
                dma((LOADS,)),
                dma((14,)),
                dma,
                dma((4,)),
                dma((4,)),
                dma((4,)),
                dma((4,)),
                dma((2, RAW_PARTS)),
                dma((2, RAW_PARTS)),
                dma((2, 8)),
                dma((2, 8)),
                dma((2, CHUNKS)),
                dma((2, CHUNKS)),
                dma((CHUNKS, 4)),
                dma((CHUNKS, 4)),
                dma((CHUNKS, 4)),
                dma((CHUNKS, 4)),
                dma((2,)),
                pltpu.SemaphoreType.REGULAR,
                pltpu.SemaphoreType.REGULAR,
            ],
        ],
        compiler_params=pltpu.CompilerParams(collective_id=0, has_side_effects=True, vmem_limit_bytes=48 << 20),
        name="jacobi_step",
    )(matrix)


def solution(mesh):
    return jax.shard_map(
        per_device, mesh=mesh, in_specs=(P("row", "pair"),), out_specs=P("row", "pair"), check_vma=False
    )
```

```python
import functools

import jax
import jax.numpy as jnp
from jax import lax
from jax.experimental import pallas as pl
from jax.experimental.pallas import tpu as pltpu
from jax.sharding import PartitionSpec as P

N = 128
D = 72
STAGES = 8
UNROLL = 16
MESH = pl.DeviceIdType.MESH
HIGH = lax.Precision.HIGHEST


def angles(a, b, g):
    d = b - a
    x = jnp.abs(d)
    y = 2.0 * g
    scale = jnp.where(jnp.maximum(x, jnp.abs(y)) < 2.0**-50, 2.0**80, 1.0)
    x = x * scale
    y = jnp.where(d < 0, -y, y) * scale
    turns = x > 0
    x = jnp.where(turns, x, 1.0)
    y = jnp.where(turns, y, 0.0)
    inv = lax.rsqrt(x * x + y * y)
    c2 = 0.5 + (0.5 * x) * inv
    inv_c = lax.rsqrt(c2)
    return c2 * inv_c, ((0.5 * y) * inv) * inv_c


def fan(x):
    return pltpu.roll(x, 0, 1, stride=1, stride_axis=0)


def fan_back(x):
    row = lax.broadcasted_iota(jnp.int32, x.shape, 0)
    for bit in (1, 2, 4):
        x = jnp.where((row & bit) != 0, pltpu.roll(x, N - bit, 1), x)
    parts = [x[m : m + 8] if m == 0 else pltpu.roll(x[m : m + 8], N - m, 1) for m in range(0, N, 8)]
    return jnp.concatenate(parts, axis=0)


def skew(transposed):
    return fan(fan_back(transposed).T)


def rounds(gram_ref, out_ref, a_ref, b_ref, g_ref, t_ref, ml_ref, mr_ref):
    cross = gram_ref[:, 0:16, :].reshape(N, N)
    packed = gram_ref[:, 16:32, :].reshape(N, N)
    row = lax.broadcasted_iota(jnp.int32, (N, N), 0)
    column = lax.broadcasted_iota(jnp.int32, (N, N), 1)
    flipped = packed.T
    right = jnp.where(row > column, packed, flipped)
    a_ref[...] = skew(jnp.where(row <= column, packed, flipped))[:D]
    b_ref[...] = skew(jnp.where(row == column, gram_ref[0, 32:33, :], right))[:D]
    g_ref[pl.ds(N, D), :] = skew(cross.T)[:D]
    t_ref[pl.ds(0, D), :] = skew(cross)[:D]
    ml_ref[...] = jnp.zeros_like(ml_ref)
    mr_ref[...] = jnp.zeros_like(mr_ref)
    ml_ref[0, pl.ds(0, 1), :] = jnp.ones((1, N), jnp.float32)
    mr_ref[1, pl.ds(N, 1), :] = jnp.ones((1, N), jnp.float32)

    def back(x, lanes):
        return pltpu.roll(x, N - lanes, 1)

    def turned(a, t, g, b, c, s, cc, ss):
        a, t = c * a - s * t, s * a + c * t
        g, b = c * g - s * b, s * g + c * b
        a, g = cc * a - ss * g, ss * a + cc * g
        t, b = cc * t - ss * b, ss * t + cc * b
        return a, t, g, b

    def full_round(rows, r, c, s):
        n = max(rows, D)
        cd = fan(jnp.broadcast_to(c, (n, N)))
        sd = fan(jnp.broadcast_to(s, (n, N)))
        gw, tw = pl.ds(N - r, D), pl.ds(r, D)
        a, t, g, b = turned(a_ref[...], t_ref[tw, :], g_ref[gw, :], b_ref[...], c, s, cd[:D], sd[:D])
        b_next, t_next = back(b, 1), back(t, 1)
        a_ref[...] = a
        b_ref[...] = b_next
        g_ref[gw, :] = g
        t_ref[tw, :] = t_next
        g_ref[pl.ds(N - 1 - r, 1), :] = t_next[1:2]
        t_ref[pl.ds(r + D, 1), :] = back(g[N - D : N - D + 1], N - D + 1)
        mw = pl.ds(N - r, rows)
        cm, sm = cd[:rows], sd[:rows]
        for h in range(2):
            left, right = ml_ref[h, pl.ds(0, rows), :], mr_ref[h, mw, :]
            ml_ref[h, pl.ds(0, rows), :] = cm * left - sm * right
            mr_ref[h, mw, :] = sm * left + cm * right
        return a, t, g, b

    def two_rounds(rows, r, carry):
        (a0, b0, g0), (a1, b1, g1), (a2, b2, g2), near, middle, far = carry
        c0, s0 = angles(a0, b0, g0)
        c1, s1, c2, s2 = back(c0, 1), back(s0, 1), back(c0, 2), back(s0, 2)
        diag0 = turned(a0, g0, g0, b0, c0, s0, c0, s0)
        diag1 = turned(a1, g1, g1, b1, c1, s1, c1, s1)
        diag2 = turned(a2, g2, g2, b2, c2, s2, c2, s2)
        near = turned(*near, c1, s1, c0, s0)
        middle = turned(*middle, c2, s2, c1, s1)
        far = turned(*far, c2, s2, c0, s0)
        full_round(rows, r, c0, s0)
        cross = diag1[2]
        a0, b0, g0 = diag0[0], diag1[3], near[1]
        a1, b1, g1 = diag1[0], diag2[3], middle[1]
        c0, s0 = angles(a0, b0, g0)
        c1, s1 = angles(a1, b1, g1)
        diag0 = turned(a0, g0, g0, b0, c0, s0, c0, s0)
        diag1 = turned(a1, g1, g1, b1, c1, s1, c1, s1)
        near = turned(near[0], far[1], cross, middle[3], c1, s1, c0, s0)
        a, t, g, b = full_round(rows, r + 1, c0, s0)
        first = (diag0[0], diag1[3], near[1])
        return (
            first,
            tuple(back(v, 1) for v in first),
            tuple(back(v, 2) for v in first),
            (back(a[1:2], 1), back(t[2:3], 2), back(g[0:1], 1), back(b[1:2], 2)),
            (back(a[1:2], 2), back(t[2:3], 3), back(g[0:1], 2), back(b[1:2], 3)),
            (back(a[2:3], 2), back(t[3:4], 3), back(g[1:2], 2), back(b[2:3], 3)),
        )

    def group(rows, i, carry):
        for u in range(0, UNROLL, 2):
            carry = two_rounds(rows, UNROLL * i + u, carry)
        return carry

    def entries(d, lanes):
        rows = (a_ref[d : d + 1, :], t_ref[d : d + 1, :], g_ref[N + d : N + d + 1, :], b_ref[d : d + 1, :])
        return tuple(back(v, lanes) for v in rows)

    first = (a_ref[0:1, :], b_ref[0:1, :], t_ref[0:1, :])
    carry = (
        first, tuple(back(v, 1) for v in first), tuple(back(v, 2) for v in first), entries(1, 1), entries(1, 2), entries(2, 2)
    )
    for stage in range(STAGES):
        begin, end = N * stage // STAGES, N * (stage + 1) // STAGES
        carry = lax.fori_loop(begin // UNROLL, end // UNROLL, functools.partial(group, end), carry)
    for h in range(2):
        mr_ref[h, pl.ds(0, 1), :] = mr_ref[h, pl.ds(N, 1), :]
        out_ref[0:N, h * N : (h + 1) * N] = fan(fan_back(ml_ref[h]).T)
        out_ref[N:, h * N : (h + 1) * N] = fan(fan_back(mr_ref[h, 0:N, :]).T)


ROUND_SCRATCH = [
    pltpu.VMEM((D, N), jnp.float32),
    pltpu.VMEM((D, N), jnp.float32),
    pltpu.VMEM((208, N), jnp.float32),
    pltpu.VMEM((208, N), jnp.float32),
    pltpu.VMEM((2, N, N), jnp.float32),
    pltpu.VMEM((2, 2 * N, N), jnp.float32),
]


EARLY = 1024
RAW_PARTS = 8
RAW_FIRST = 0
CHUNK = 256
CHUNKS = 8
QUARTER = CHUNK // 4
ORDER = tuple(range(EARLY // CHUNK, CHUNKS)) + tuple(range(EARLY // CHUNK))
LOADS = 2


def remote(src, dst, send_sem, recv_sem, to):
    return pltpu.make_async_remote_copy(
        src_ref=src, dst_ref=dst, send_sem=send_sem, recv_sem=recv_sem, device_id=to, device_id_type=MESH
    )


def mixed(rows, mixing):
    return lax.dot_general(
        rows, mixing, (((1,), (1,)), ((), ())), precision=HIGH, preferred_element_type=jnp.float32
    )


def partial_gram(x_ref, xb, part, load):
    size = xb.shape[0] // LOADS
    copies = []
    for j in range(LOADS):
        at = pl.ds(j * size, size)
        copies.append(pltpu.make_async_copy(x_ref.at[at], xb.at[at], load.at[j]))
        copies[-1].start()

    def cross(u, v):
        return lax.dot_general(u, v, (((0,), (0,)), ((), ())), preferred_element_type=jnp.float32)

    even = odd = 0.0
    for j in range(LOADS):
        copies[j].wait()
        x = xb[pl.ds(j * size, size), :]
        high = x.astype(jnp.bfloat16)
        rest = x - high.astype(jnp.float32)
        mid = rest.astype(jnp.bfloat16)
        low = (rest - mid.astype(jnp.float32)).astype(jnp.bfloat16)
        even = even + (cross(high, high) + cross(mid, mid))
        odd = odd + (cross(high, mid) + cross(high, low))
    gram = even + (odd + odd.T)
    row = lax.broadcasted_iota(jnp.int32, (N, N), 0)
    column = lax.broadcasted_iota(jnp.int32, (N, N), 1)
    packed = jnp.where(row <= column, gram[:N, :N], gram[N:, N:])
    diagonal = jnp.sum(jnp.where(row == column, gram[N:, N:], 0.0), axis=0, keepdims=True)
    for e in range(8):
        part[e, 0:16] = gram[16 * e : 16 * e + 16, N:]
        part[e, 16:32] = packed[16 * e : 16 * e + 16]
        part[e, 32:33] = diagonal if e == 0 else jnp.zeros_like(diagonal)


def step_kernel(x_ref, out_ref, xb, y, raw, raw_y, relay, part, half, total, in_core, in_x, in_z, mix, near, round_refs, sems):
    me, k = lax.axis_index("row"), lax.axis_index("pair")
    core, x, z = lax.rem(me, 2), lax.rem(me // 2, 4), me // 8
    last = lax.axis_size("pair") - 1
    py, pz = k // 4, lax.rem(k, 4)
    to_after, to_before = pz < 3, pz > 0

    def pair(distance):
        return {"pair": lax.rem(k + distance + last + 1, last + 1)}

    after, before = pair(1), pair(-1)
    top = pz == 3
    edge = top | (pz == 0)
    wraps = (top & (py < 3)) | ((pz == 0) & (py > 0))
    step = jnp.where(top, 1, -1)
    direct_mine = jnp.where(top, 3 - py, py)
    direct_passed = jnp.where(top, 4 - py, py + 1)
    column_mine = pl.ds(pl.multiple_of(jnp.where(top, 0, N), N), N)
    column_here = pl.ds(pl.multiple_of(jnp.where(top, N, 0), N), N)
    half_mine = jnp.where(top, 0, 1)
    load, send, recv_core, recv_x, recv_z, recv_gx, recv_gc, raw_send, raw_recv, mix_send, mix_recv, late_send, late_recv, wrap_send, wrap_recv, relay_send, relay_recv, keep, near_ready, far_ready = sems

    def place(z, x, core):
        return {"row": (z * 4 + x) * 2 + core}

    def peer(i):
        other = lax.rem(me + i, 8)
        return other, {"row": z * 8 + other}

    barrier = pltpu.get_barrier_semaphore()

    def chip(distance, core):
        return {"pair": lax.rem(k + distance + last + 1, last + 1), "row": (z * 4 + x) * 2 + core}

    def exists(distance):
        return (k + distance >= 0) & (k + distance <= last)

    pairs = [
        (1, exists(1)), (-1, exists(-1)), (4, edge & exists(4)), (-4, edge & exists(-4)), (3, pz == 0), (-3, top),
    ]
    hears = 7
    for distance, there in pairs:
        hears = hears + 2 * there.astype(jnp.int32)

    def call(to):
        pl.semaphore_signal(barrier, inc=1, device_id=to, device_id_type=MESH)

    pl.when(core == 1)(lambda: call(place(z, x, 0)))
    for i in range(1, 4):
        call(place(lax.rem(z + i, 4), x, 1))
    for i in range(1, 4):
        call(place(z, lax.rem(x + i, 4), 0))
    for distance, there in pairs:
        pl.when(there)(lambda: call(chip(distance, 0)))

    partial_gram(x_ref, xb, part, load)

    @pl.when(core == 0)
    def _():
        pl.semaphore_wait(barrier, hears)
        pl.semaphore_signal(near_ready, inc=1, device_id=place(z, x, 1), device_id_type=MESH)

    pl.when(core == 1)(lambda: pl.semaphore_wait(near_ready, 1))

    mine = pl.ds(core * 4, 4)
    other = pl.ds((1 - core) * 4, 4)
    sent = []
    c = remote(part.at[other], in_core, send.at[0], recv_core, place(z, x, 1 - core))
    c.start()
    sent.append(c)

    size = EARLY // RAW_PARTS
    raw_f, raw_b = [], []
    for j in range(RAW_PARTS):
        at = pl.ds(j * size, size)
        raw_f.append(remote(xb.at[at], raw.at[0, at], raw_send.at[0, j], raw_recv.at[0, j], after))
        raw_b.append(remote(xb.at[at], raw.at[1, at], raw_send.at[1, j], raw_recv.at[1, j], before))

    def start_raw(begin, end):
        for j in range(begin, end):
            pl.when(to_after)(raw_f[j].start)
            pl.when(to_before)(raw_b[j].start)

    start_raw(0, RAW_FIRST)
    c.wait_recv()
    half[...] = part[mine] + in_core[...]

    for i in range(1, 4):
        xt = lax.rem(x + i, 4)
        c = remote(half.at[xt], in_x.at[x], send.at[i], recv_x.at[x], place(z, xt, core))
        c.start()
        sent.append(c)
    in_x[x] = half[x]
    for i in range(1, 4):
        xf = lax.rem(x + i, 4)
        remote(in_x.at[xf], in_x.at[xf], send.at[i], recv_x.at[xf], place(z, xf, core)).wait_recv()
    in_z[z] = (in_x[0] + in_x[1]) + (in_x[2] + in_x[3])

    @pl.when(core == 1)
    def _():
        pl.semaphore_wait(barrier, 6)
        pl.semaphore_signal(far_ready, inc=1, device_id=place(z, x, 0), device_id_type=MESH)

    pl.when(core == 0)(lambda: pl.semaphore_wait(far_ready, 1))
    for i in range(1, 4):
        zt = lax.rem(z + i, 4)
        c = remote(in_z.at[z], in_z.at[z], send.at[3 + i], recv_z.at[z], place(zt, x, core))
        c.start()
        sent.append(c)
    for i in range(1, 4):
        zf = lax.rem(z + i, 4)
        remote(in_z.at[zf], in_z.at[zf], send.at[3 + i], recv_z.at[zf], place(zf, x, core)).wait_recv()

    def rows_of(core, x):
        return total.at[core * 4 + x]

    own = rows_of(core, x)
    own[...] = (in_z[0] + in_z[1]) + (in_z[2] + in_z[3])
    for i in range(1, 4):
        c = remote(own, own, send.at[6 + i], recv_gx.at[x], place(z, lax.rem(x + i, 4), core))
        c.start()
        sent.append(c)
    start_raw(RAW_FIRST, RAW_PARTS)
    for i in range(4):
        xf = lax.rem(x + i, 4)
        there = rows_of(core, xf)
        if i:
            remote(there, there, send.at[6 + i], recv_gx.at[xf], place(z, xf, core)).wait_recv()
        c = remote(there, there, send.at[10 + i], recv_gc.at[xf], place(z, x, 1 - core))
        c.start()
        sent.append(c)
    for i in range(4):
        xf = lax.rem(x + i, 4)
        there = rows_of(1 - core, xf)
        remote(there, there, send.at[10 + i], recv_gc.at[xf], place(z, x, 1 - core)).wait_recv()
    for c in sent:
        c.wait_send()

    rounds(total, mix, *round_refs)

    seat = lax.rem(me, 8)
    share = N // 8

    def eighth(i):
        return pl.ds(pl.multiple_of(i * share, 8), share)

    first = jnp.where(k == 0, N, 0)
    mix_f = remote(
        mix.at[pl.ds(pl.multiple_of(first + seat * share, 8), share)], near.at[0, eighth(seat)],
        mix_send.at[0, 0], mix_recv.at[0, seat], after,
    )
    mix_b = remote(
        mix.at[pl.ds(pl.multiple_of(N + seat * share, 8), share)], near.at[1, eighth(seat)],
        mix_send.at[1, 0], mix_recv.at[1, seat], before,
    )
    pl.when(to_after)(mix_f.start)
    pl.when(to_before)(mix_b.start)

    def chunk(c):
        return pl.ds(c * CHUNK, CHUNK)

    def late_f(c):
        src = y.at[jnp.where(k == 0, 1, 0), chunk(c)]
        return remote(src, out_ref.at[chunk(c), pl.ds(0, N)], late_send.at[0, c], late_recv.at[0, c], after)

    def late_b(c):
        return remote(y.at[1, chunk(c)], out_ref.at[chunk(c), pl.ds(N, N)], late_send.at[1, c], late_recv.at[1, c], before)

    def rows_at(c, i):
        return pl.ds(c * CHUNK + i * QUARTER, QUARTER)

    def wrap_direct(c, i):
        at = rows_at(c, i)
        return remote(y.at[half_mine, at], out_ref.at[at, column_mine], wrap_send.at[c, i], wrap_recv.at[c, i], pair(step))

    def wrap_aside(c, i):
        at = rows_at(c, i)
        return remote(y.at[half_mine, at], relay.at[c, i - 1], wrap_send.at[c, i], relay_recv.at[c, i], pair(4 * step))

    def wrap_passed(c, i):
        dst = out_ref.at[rows_at(c, i), column_mine]
        return remote(relay.at[c, i - 1], dst, relay_send.at[c, i], wrap_recv.at[c, i], pair(-3 * step))

    def wrap_here(c, i):
        dst = out_ref.at[rows_at(c, i), column_here]
        return remote(y.at[half_mine, rows_at(c, i)], dst, wrap_send.at[c, i], wrap_recv.at[c, i], pair(step))

    def rotate(c):
        moved = mixed(xb[chunk(c), :], mix[...])
        y[0, chunk(c)] = moved[:, :N]
        y[1, chunk(c)] = moved[:, N:]

    def send_aside(c):
        for i in range(1, 4):
            pl.when(wraps & (i >= direct_mine))(wrap_aside(c, i).start)

    for c in ORDER:
        if c * CHUNK >= EARLY:
            rotate(c)
            send_aside(c)
            pl.when(to_after)(late_f(c).start)
            pl.when(to_before)(late_b(c).start)
        else:

            @pl.when(edge)
            def _():
                rotate(c)
                send_aside(c)

    for c in ORDER:
        for i in range(3):
            pl.when(wraps & (i < direct_mine))(wrap_direct(c, i).start)

    keep_left = pltpu.make_async_copy(y.at[0], out_ref.at[:, pl.ds(0, N)], keep.at[0])
    keep_right = pltpu.make_async_copy(y.at[0], out_ref.at[:, pl.ds(N, N)], keep.at[1])
    pl.when(k == 0)(keep_left.start)
    pl.when(k == last)(keep_right.start)

    def pass_on(c):
        for i in range(1, 4):

            @pl.when(edge & (i >= direct_passed))
            def _():
                wrap_aside(c, i).wait_recv()
                wrap_passed(c, i).start()

    def spread(which, first):
        first.wait_recv()
        for i in range(1, 8):
            slot = near.at[which, eighth(seat)]
            remote(slot, slot, mix_send.at[which, i], mix_recv.at[which, seat], peer(i)[1]).start()

    def early(which):
        return pltpu.make_async_copy(
            raw_y.at[which], out_ref.at[pl.ds(0, EARLY), pl.ds(which * N, N)], keep.at[which]
        )

    def finish(which, copies):
        for c in copies:
            c.wait_recv()
        for i in range(1, 8):
            there, device = peer(i)
            slot = near.at[which, eighth(there)]
            remote(slot, slot, mix_send.at[which, i], mix_recv.at[which, there], device).wait_recv()
        for c in range(EARLY // CHUNK):
            raw_y[which, chunk(c)] = mixed(raw[which, chunk(c)], near[which])
        early(which).start()

    pl.when(to_before)(lambda: spread(0, mix_f))
    pl.when(to_after)(lambda: spread(1, mix_b))
    for c in ORDER:
        pass_on(c)
    pl.when(to_before)(lambda: finish(0, raw_f))
    pl.when(to_after)(lambda: finish(1, raw_b))

    def sent_mix(which):
        for i in range(1, 8):
            slot = near.at[which, eighth(seat)]
            remote(slot, slot, mix_send.at[which, i], mix_recv.at[which, seat], peer(i)[1]).wait_send()

    late = [c for c in ORDER if c * CHUNK >= EARLY]

    @pl.when(to_after)
    def _():
        for c in [mix_f] + raw_f + [late_f(c) for c in late]:
            c.wait_send()
        for c in late:
            late_b(c).wait_recv()
        sent_mix(1)
        early(1).wait()

    @pl.when(to_before)
    def _():
        for c in [mix_b] + raw_b + [late_b(c) for c in late]:
            c.wait_send()
        for c in late:
            late_f(c).wait_recv()
        sent_mix(0)
        early(0).wait()

    for c in ORDER:
        for i in range(4):

            @pl.when(wraps)
            def _():
                wrap_here(c, i).wait_send()
                wrap_here(c, i).wait_recv()

            if i:
                pl.when(edge & (i >= direct_passed))(wrap_passed(c, i).wait_send)
    pl.when(k == 0)(keep_left.wait)
    pl.when(k == last)(keep_right.wait)


def per_device(matrix):
    rows = matrix.shape[0]
    eighth = (33, N)
    dma = pltpu.SemaphoreType.DMA
    f32 = jnp.float32
    return pl.pallas_call(
        step_kernel,
        out_shape=jax.ShapeDtypeStruct(matrix.shape, f32),
        in_specs=[pl.BlockSpec(memory_space=pltpu.HBM)],
        out_specs=pl.BlockSpec(memory_space=pl.ANY),
        scratch_shapes=[
            pltpu.VMEM((rows, 2 * N), f32),
            pltpu.VMEM((2, rows, N), f32),
            pltpu.VMEM((2, EARLY, 2 * N), f32),
            pltpu.VMEM((2, EARLY, N), f32),
            pltpu.VMEM((CHUNKS, 3, QUARTER, N), f32),
            pltpu.VMEM((8, *eighth), f32),
            pltpu.VMEM((4, *eighth), f32),
            pltpu.VMEM((8, *eighth), f32),
            pltpu.VMEM((4, *eighth), f32),
            pltpu.VMEM((4, *eighth), f32),
            pltpu.VMEM((4, *eighth), f32),
            pltpu.VMEM((2 * N, 2 * N), f32),
            pltpu.VMEM((2, N, 2 * N), f32),
            ROUND_SCRATCH,
            [
                dma((LOADS,)),
                dma((14,)),
                dma,
                dma((4,)),
                dma((4,)),
                dma((4,)),
                dma((4,)),
                dma((2, RAW_PARTS)),
                dma((2, RAW_PARTS)),
                dma((2, 8)),
                dma((2, 8)),
                dma((2, CHUNKS)),
                dma((2, CHUNKS)),
                dma((CHUNKS, 4)),
                dma((CHUNKS, 4)),
                dma((CHUNKS, 4)),
                dma((CHUNKS, 4)),
                dma((2,)),
                pltpu.SemaphoreType.REGULAR,
                pltpu.SemaphoreType.REGULAR,
            ],
        ],
        compiler_params=pltpu.CompilerParams(collective_id=0, has_side_effects=True, vmem_limit_bytes=48 << 20),
        name="jacobi_step",
    )(matrix)


def solution(mesh):
    return jax.shard_map(
        per_device, mesh=mesh, in_specs=(P("row", "pair"),), out_specs=P("row", "pair"), check_vma=False
    )
```

```python
import functools

import jax
import jax.numpy as jnp
from jax import lax
from jax.experimental import pallas as pl
from jax.experimental.pallas import tpu as pltpu
from jax.sharding import PartitionSpec as P

N = 128
D = 72
STAGES = 8
UNROLL = 16
MESH = pl.DeviceIdType.MESH
HIGH = lax.Precision.HIGHEST


def angles(a, b, g):
    d = b - a
    x = jnp.abs(d)
    y = 2.0 * g
    scale = jnp.where(jnp.maximum(x, jnp.abs(y)) < 2.0**-50, 2.0**80, 1.0)
    x = x * scale
    y = jnp.where(d < 0, -y, y) * scale
    turns = x > 0
    x = jnp.where(turns, x, 1.0)
    y = jnp.where(turns, y, 0.0)
    inv = lax.rsqrt(x * x + y * y)
    c2 = 0.5 + (0.5 * x) * inv
    inv_c = lax.rsqrt(c2)
    return c2 * inv_c, ((0.5 * y) * inv) * inv_c


def fan(x):
    return pltpu.roll(x, 0, 1, stride=1, stride_axis=0)


def fan_back(x):
    row = lax.broadcasted_iota(jnp.int32, x.shape, 0)
    for bit in (1, 2, 4):
        x = jnp.where((row & bit) != 0, pltpu.roll(x, N - bit, 1), x)
    parts = [x[m : m + 8] if m == 0 else pltpu.roll(x[m : m + 8], N - m, 1) for m in range(0, N, 8)]
    return jnp.concatenate(parts, axis=0)


def skew(transposed):
    return fan(fan_back(transposed).T)


def rounds(gram_ref, out_ref, a_ref, b_ref, g_ref, t_ref, ml_ref, mr_ref):
    cross = gram_ref[:, 0:16, :].reshape(N, N)
    packed = gram_ref[:, 16:32, :].reshape(N, N)
    row = lax.broadcasted_iota(jnp.int32, (N, N), 0)
    column = lax.broadcasted_iota(jnp.int32, (N, N), 1)
    flipped = packed.T
    right = jnp.where(row > column, packed, flipped)
    a_ref[...] = skew(jnp.where(row <= column, packed, flipped))[:D]
    b_ref[...] = skew(jnp.where(row == column, gram_ref[0, 32:33, :], right))[:D]
    g_ref[pl.ds(N, D), :] = skew(cross.T)[:D]
    t_ref[pl.ds(0, D), :] = skew(cross)[:D]
    ml_ref[...] = jnp.zeros_like(ml_ref)
    mr_ref[...] = jnp.zeros_like(mr_ref)
    ml_ref[0, pl.ds(0, 1), :] = jnp.ones((1, N), jnp.float32)
    mr_ref[1, pl.ds(N, 1), :] = jnp.ones((1, N), jnp.float32)

    def back(x, lanes):
        return pltpu.roll(x, N - lanes, 1)

    def turned(a, t, g, b, c, s, cc, ss):
        a, t = c * a - s * t, s * a + c * t
        g, b = c * g - s * b, s * g + c * b
        a, g = cc * a - ss * g, ss * a + cc * g
        t, b = cc * t - ss * b, ss * t + cc * b
        return a, t, g, b

    def full_round(rows, r, c, s):
        n = max(rows, D)
        cd = fan(jnp.broadcast_to(c, (n, N)))
        sd = fan(jnp.broadcast_to(s, (n, N)))
        gw, tw = pl.ds(N - r, D), pl.ds(r, D)
        a, t, g, b = turned(a_ref[...], t_ref[tw, :], g_ref[gw, :], b_ref[...], c, s, cd[:D], sd[:D])
        b_next, t_next = back(b, 1), back(t, 1)
        a_ref[...] = a
        b_ref[...] = b_next
        g_ref[gw, :] = g
        t_ref[tw, :] = t_next
        g_ref[pl.ds(N - 1 - r, 1), :] = t_next[1:2]
        t_ref[pl.ds(r + D, 1), :] = back(g[N - D : N - D + 1], N - D + 1)
        mw = pl.ds(N - r, rows)
        cm, sm = cd[:rows], sd[:rows]
        for h in range(2):
            left, right = ml_ref[h, pl.ds(0, rows), :], mr_ref[h, mw, :]
            ml_ref[h, pl.ds(0, rows), :] = cm * left - sm * right
            mr_ref[h, mw, :] = sm * left + cm * right
        return a, t, g, b

    def two_rounds(rows, r, carry):
        (a0, b0, g0), (a1, b1, g1), (a2, b2, g2), near, middle, far = carry
        c0, s0 = angles(a0, b0, g0)
        c1, s1, c2, s2 = back(c0, 1), back(s0, 1), back(c0, 2), back(s0, 2)
        diag0 = turned(a0, g0, g0, b0, c0, s0, c0, s0)
        diag1 = turned(a1, g1, g1, b1, c1, s1, c1, s1)
        diag2 = turned(a2, g2, g2, b2, c2, s2, c2, s2)
        near = turned(*near, c1, s1, c0, s0)
        middle = turned(*middle, c2, s2, c1, s1)
        far = turned(*far, c2, s2, c0, s0)
        full_round(rows, r, c0, s0)
        cross = diag1[2]
        a0, b0, g0 = diag0[0], diag1[3], near[1]
        a1, b1, g1 = diag1[0], diag2[3], middle[1]
        c0, s0 = angles(a0, b0, g0)
        c1, s1 = angles(a1, b1, g1)
        diag0 = turned(a0, g0, g0, b0, c0, s0, c0, s0)
        diag1 = turned(a1, g1, g1, b1, c1, s1, c1, s1)
        near = turned(near[0], far[1], cross, middle[3], c1, s1, c0, s0)
        a, t, g, b = full_round(rows, r + 1, c0, s0)
        first = (diag0[0], diag1[3], near[1])
        return (
            first,
            tuple(back(v, 1) for v in first),
            tuple(back(v, 2) for v in first),
            (back(a[1:2], 1), back(t[2:3], 2), back(g[0:1], 1), back(b[1:2], 2)),
            (back(a[1:2], 2), back(t[2:3], 3), back(g[0:1], 2), back(b[1:2], 3)),
            (back(a[2:3], 2), back(t[3:4], 3), back(g[1:2], 2), back(b[2:3], 3)),
        )

    def group(rows, i, carry):
        for u in range(0, UNROLL, 2):
            carry = two_rounds(rows, UNROLL * i + u, carry)
        return carry

    def entries(d, lanes):
        rows = (a_ref[d : d + 1, :], t_ref[d : d + 1, :], g_ref[N + d : N + d + 1, :], b_ref[d : d + 1, :])
        return tuple(back(v, lanes) for v in rows)

    first = (a_ref[0:1, :], b_ref[0:1, :], t_ref[0:1, :])
    carry = (
        first, tuple(back(v, 1) for v in first), tuple(back(v, 2) for v in first), entries(1, 1), entries(1, 2), entries(2, 2)
    )
    for stage in range(STAGES):
        begin, end = N * stage // STAGES, N * (stage + 1) // STAGES
        carry = lax.fori_loop(begin // UNROLL, end // UNROLL, functools.partial(group, end), carry)
    for h in range(2):
        mr_ref[h, pl.ds(0, 1), :] = mr_ref[h, pl.ds(N, 1), :]
        out_ref[0:N, h * N : (h + 1) * N] = fan(fan_back(ml_ref[h]).T)
        out_ref[N:, h * N : (h + 1) * N] = fan(fan_back(mr_ref[h, 0:N, :]).T)


ROUND_SCRATCH = [
    pltpu.VMEM((D, N), jnp.float32),
    pltpu.VMEM((D, N), jnp.float32),
    pltpu.VMEM((208, N), jnp.float32),
    pltpu.VMEM((208, N), jnp.float32),
    pltpu.VMEM((2, N, N), jnp.float32),
    pltpu.VMEM((2, 2 * N, N), jnp.float32),
]


EARLY = 1024
RAW_PARTS = 8
RAW_FIRST = 0
CHUNK = 256
CHUNKS = 8
QUARTER = CHUNK // 4
ORDER = tuple(range(EARLY // CHUNK, CHUNKS)) + tuple(range(EARLY // CHUNK))
LOADS = 2


def remote(src, dst, send_sem, recv_sem, to):
    return pltpu.make_async_remote_copy(
        src_ref=src, dst_ref=dst, send_sem=send_sem, recv_sem=recv_sem, device_id=to, device_id_type=MESH
    )


def mixed(rows, mixing):
    return lax.dot_general(
        rows, mixing, (((1,), (1,)), ((), ())), precision=HIGH, preferred_element_type=jnp.float32
    )


def partial_gram(x_ref, xb, part, load):
    size = xb.shape[0] // LOADS
    copies = []
    for j in range(LOADS):
        at = pl.ds(j * size, size)
        copies.append(pltpu.make_async_copy(x_ref.at[at], xb.at[at], load.at[j]))
        copies[-1].start()

    def cross(u, v):
        return lax.dot_general(u, v, (((0,), (0,)), ((), ())), preferred_element_type=jnp.float32)

    even = odd = 0.0
    for j in range(LOADS):
        copies[j].wait()
        x = xb[pl.ds(j * size, size), :]
        high = x.astype(jnp.bfloat16)
        rest = x - high.astype(jnp.float32)
        mid = rest.astype(jnp.bfloat16)
        low = (rest - mid.astype(jnp.float32)).astype(jnp.bfloat16)
        even = even + (cross(high, high) + cross(mid, mid))
        odd = odd + (cross(high, mid) + cross(high, low))
    gram = even + (odd + odd.T)
    row = lax.broadcasted_iota(jnp.int32, (N, N), 0)
    column = lax.broadcasted_iota(jnp.int32, (N, N), 1)
    packed = jnp.where(row <= column, gram[:N, :N], gram[N:, N:])
    diagonal = jnp.sum(jnp.where(row == column, gram[N:, N:], 0.0), axis=0, keepdims=True)
    for e in range(8):
        part[e, 0:16] = gram[16 * e : 16 * e + 16, N:]
        part[e, 16:32] = packed[16 * e : 16 * e + 16]
        part[e, 32:33] = diagonal if e == 0 else jnp.zeros_like(diagonal)


def step_kernel(x_ref, out_ref, xb, y, raw, raw_y, relay, part, half, total, in_core, in_x, in_z, mix, near, round_refs, sems):
    me, k = lax.axis_index("row"), lax.axis_index("pair")
    core, x, z = lax.rem(me, 2), lax.rem(me // 2, 4), me // 8
    last = lax.axis_size("pair") - 1
    py, pz = k // 4, lax.rem(k, 4)
    to_after, to_before = pz < 3, pz > 0

    def pair(distance):
        return {"pair": lax.rem(k + distance + last + 1, last + 1)}

    after, before = pair(1), pair(-1)
    top = pz == 3
    edge = top | (pz == 0)
    wraps = (top & (py < 3)) | ((pz == 0) & (py > 0))
    step = jnp.where(top, 1, -1)
    direct_mine = jnp.where(top, 3 - py, py)
    direct_passed = jnp.where(top, 4 - py, py + 1)
    column_mine = pl.ds(pl.multiple_of(jnp.where(top, 0, N), N), N)
    column_here = pl.ds(pl.multiple_of(jnp.where(top, N, 0), N), N)
    half_mine = jnp.where(top, 0, 1)
    load, send, recv_core, recv_x, recv_z, recv_gx, recv_gc, raw_send, raw_recv, mix_send, mix_recv, late_send, late_recv, wrap_send, wrap_recv, relay_send, relay_recv, keep, near_ready, far_ready = sems

    def place(z, x, core):
        return {"row": (z * 4 + x) * 2 + core}

    def peer(i):
        other = lax.rem(me + i, 8)
        return other, {"row": z * 8 + other}

    barrier = pltpu.get_barrier_semaphore()

    def chip(distance, core):
        return {"pair": lax.rem(k + distance + last + 1, last + 1), "row": (z * 4 + x) * 2 + core}

    def exists(distance):
        return (k + distance >= 0) & (k + distance <= last)

    pairs = [
        (1, exists(1)), (-1, exists(-1)), (4, edge & exists(4)), (-4, edge & exists(-4)), (3, pz == 0), (-3, top),
    ]
    hears = 7
    for distance, there in pairs:
        hears = hears + 2 * there.astype(jnp.int32)

    def call(to):
        pl.semaphore_signal(barrier, inc=1, device_id=to, device_id_type=MESH)

    pl.when(core == 1)(lambda: call(place(z, x, 0)))
    for i in range(1, 4):
        call(place(lax.rem(z + i, 4), x, 1))
    for i in range(1, 4):
        call(place(z, lax.rem(x + i, 4), 0))
    for distance, there in pairs:
        pl.when(there)(lambda: call(chip(distance, 0)))

    partial_gram(x_ref, xb, part, load)

    @pl.when(core == 0)
    def _():
        pl.semaphore_wait(barrier, hears)
        pl.semaphore_signal(near_ready, inc=1, device_id=place(z, x, 1), device_id_type=MESH)

    pl.when(core == 1)(lambda: pl.semaphore_wait(near_ready, 1))

    mine = pl.ds(core * 4, 4)
    other = pl.ds((1 - core) * 4, 4)
    sent = []
    c = remote(part.at[other], in_core, send.at[0], recv_core, place(z, x, 1 - core))
    c.start()
    sent.append(c)

    size = EARLY // RAW_PARTS
    raw_f, raw_b = [], []
    for j in range(RAW_PARTS):
        at = pl.ds(j * size, size)
        raw_f.append(remote(xb.at[at], raw.at[0, at], raw_send.at[0, j], raw_recv.at[0, j], after))
        raw_b.append(remote(xb.at[at], raw.at[1, at], raw_send.at[1, j], raw_recv.at[1, j], before))

    def start_raw(begin, end):
        for j in range(begin, end):
            pl.when(to_after)(raw_f[j].start)
            pl.when(to_before)(raw_b[j].start)

    start_raw(0, RAW_FIRST)
    c.wait_recv()
    half[...] = part[mine] + in_core[...]

    for i in range(1, 4):
        xt = lax.rem(x + i, 4)
        c = remote(half.at[xt], in_x.at[x], send.at[i], recv_x.at[x], place(z, xt, core))
        c.start()
        sent.append(c)
    in_x[x] = half[x]
    for i in range(1, 4):
        xf = lax.rem(x + i, 4)
        remote(in_x.at[xf], in_x.at[xf], send.at[i], recv_x.at[xf], place(z, xf, core)).wait_recv()
    in_z[z] = (in_x[0] + in_x[1]) + (in_x[2] + in_x[3])

    @pl.when(core == 1)
    def _():
        pl.semaphore_wait(barrier, 6)
        pl.semaphore_signal(far_ready, inc=1, device_id=place(z, x, 0), device_id_type=MESH)

    pl.when(core == 0)(lambda: pl.semaphore_wait(far_ready, 1))
    for i in range(1, 4):
        zt = lax.rem(z + i, 4)
        c = remote(in_z.at[z], in_z.at[z], send.at[3 + i], recv_z.at[z], place(zt, x, core))
        c.start()
        sent.append(c)
    for i in range(1, 4):
        zf = lax.rem(z + i, 4)
        remote(in_z.at[zf], in_z.at[zf], send.at[3 + i], recv_z.at[zf], place(zf, x, core)).wait_recv()

    def rows_of(core, x):
        return total.at[core * 4 + x]

    own = rows_of(core, x)
    own[...] = (in_z[0] + in_z[1]) + (in_z[2] + in_z[3])
    for i in range(1, 4):
        c = remote(own, own, send.at[6 + i], recv_gx.at[x], place(z, lax.rem(x + i, 4), core))
        c.start()
        sent.append(c)
    start_raw(RAW_FIRST, RAW_PARTS)
    for i in range(4):
        xf = lax.rem(x + i, 4)
        there = rows_of(core, xf)
        if i:
            remote(there, there, send.at[6 + i], recv_gx.at[xf], place(z, xf, core)).wait_recv()
        c = remote(there, there, send.at[10 + i], recv_gc.at[xf], place(z, x, 1 - core))
        c.start()
        sent.append(c)
    for i in range(4):
        xf = lax.rem(x + i, 4)
        there = rows_of(1 - core, xf)
        remote(there, there, send.at[10 + i], recv_gc.at[xf], place(z, x, 1 - core)).wait_recv()
    rounds(total, mix, *round_refs)
    for c in sent:
        c.wait_send()

    seat = lax.rem(me, 8)
    share = N // 8

    def eighth(i):
        return pl.ds(pl.multiple_of(i * share, 8), share)

    first = jnp.where(k == 0, N, 0)
    mix_f = remote(
        mix.at[pl.ds(pl.multiple_of(first + seat * share, 8), share)], near.at[0, eighth(seat)],
        mix_send.at[0, 0], mix_recv.at[0, seat], after,
    )
    mix_b = remote(
        mix.at[pl.ds(pl.multiple_of(N + seat * share, 8), share)], near.at[1, eighth(seat)],
        mix_send.at[1, 0], mix_recv.at[1, seat], before,
    )
    pl.when(to_after)(mix_f.start)
    pl.when(to_before)(mix_b.start)

    def chunk(c):
        return pl.ds(c * CHUNK, CHUNK)

    def late_f(c):
        src = y.at[jnp.where(k == 0, 1, 0), chunk(c)]
        return remote(src, out_ref.at[chunk(c), pl.ds(0, N)], late_send.at[0, c], late_recv.at[0, c], after)

    def late_b(c):
        return remote(y.at[1, chunk(c)], out_ref.at[chunk(c), pl.ds(N, N)], late_send.at[1, c], late_recv.at[1, c], before)

    def rows_at(c, i):
        return pl.ds(c * CHUNK + i * QUARTER, QUARTER)

    def wrap_direct(c, i):
        at = rows_at(c, i)
        return remote(y.at[half_mine, at], out_ref.at[at, column_mine], wrap_send.at[c, i], wrap_recv.at[c, i], pair(step))

    def wrap_aside(c, i):
        at = rows_at(c, i)
        return remote(y.at[half_mine, at], relay.at[c, i - 1], wrap_send.at[c, i], relay_recv.at[c, i], pair(4 * step))

    def wrap_passed(c, i):
        dst = out_ref.at[rows_at(c, i), column_mine]
        return remote(relay.at[c, i - 1], dst, relay_send.at[c, i], wrap_recv.at[c, i], pair(-3 * step))

    def wrap_here(c, i):
        dst = out_ref.at[rows_at(c, i), column_here]
        return remote(y.at[half_mine, rows_at(c, i)], dst, wrap_send.at[c, i], wrap_recv.at[c, i], pair(step))

    def rotate(c):
        moved = mixed(xb[chunk(c), :], mix[...])
        y[0, chunk(c)] = moved[:, :N]
        y[1, chunk(c)] = moved[:, N:]

    def send_aside(c):
        for i in range(1, 4):
            pl.when(wraps & (i >= direct_mine))(wrap_aside(c, i).start)

    for c in ORDER:
        if c * CHUNK >= EARLY:
            rotate(c)
            send_aside(c)
            pl.when(to_after)(late_f(c).start)
            pl.when(to_before)(late_b(c).start)
        else:

            @pl.when(edge)
            def _():
                rotate(c)
                send_aside(c)

    for c in ORDER:
        for i in range(3):
            pl.when(wraps & (i < direct_mine))(wrap_direct(c, i).start)

    keep_left = pltpu.make_async_copy(y.at[0], out_ref.at[:, pl.ds(0, N)], keep.at[0])
    keep_right = pltpu.make_async_copy(y.at[0], out_ref.at[:, pl.ds(N, N)], keep.at[1])
    pl.when(k == 0)(keep_left.start)
    pl.when(k == last)(keep_right.start)

    def pass_on(c):
        for i in range(1, 4):

            @pl.when(edge & (i >= direct_passed))
            def _():
                wrap_aside(c, i).wait_recv()
                wrap_passed(c, i).start()

    def spread(which, first):
        first.wait_recv()
        for i in range(1, 8):
            slot = near.at[which, eighth(seat)]
            remote(slot, slot, mix_send.at[which, i], mix_recv.at[which, seat], peer(i)[1]).start()

    def early(which):
        return pltpu.make_async_copy(
            raw_y.at[which], out_ref.at[pl.ds(0, EARLY), pl.ds(which * N, N)], keep.at[which]
        )

    def finish(which, copies):
        for c in copies:
            c.wait_recv()
        for i in range(1, 8):
            there, device = peer(i)
            slot = near.at[which, eighth(there)]
            remote(slot, slot, mix_send.at[which, i], mix_recv.at[which, there], device).wait_recv()
        for c in range(EARLY // CHUNK):
            raw_y[which, chunk(c)] = mixed(raw[which, chunk(c)], near[which])
        early(which).start()

    pl.when(to_before)(lambda: spread(0, mix_f))
    pl.when(to_after)(lambda: spread(1, mix_b))
    for c in ORDER:
        pass_on(c)
    pl.when(to_before)(lambda: finish(0, raw_f))
    pl.when(to_after)(lambda: finish(1, raw_b))

    def sent_mix(which):
        for i in range(1, 8):
            slot = near.at[which, eighth(seat)]
            remote(slot, slot, mix_send.at[which, i], mix_recv.at[which, seat], peer(i)[1]).wait_send()

    late = [c for c in ORDER if c * CHUNK >= EARLY]

    @pl.when(to_after)
    def _():
        for c in [mix_f] + raw_f + [late_f(c) for c in late]:
            c.wait_send()
        for c in late:
            late_b(c).wait_recv()
        sent_mix(1)
        early(1).wait()

    @pl.when(to_before)
    def _():
        for c in [mix_b] + raw_b + [late_b(c) for c in late]:
            c.wait_send()
        for c in late:
            late_f(c).wait_recv()
        sent_mix(0)
        early(0).wait()

    for c in ORDER:
        for i in range(4):

            @pl.when(wraps)
            def _():
                wrap_here(c, i).wait_send()
                wrap_here(c, i).wait_recv()

            if i:
                pl.when(edge & (i >= direct_passed))(wrap_passed(c, i).wait_send)
    pl.when(k == 0)(keep_left.wait)
    pl.when(k == last)(keep_right.wait)


def per_device(matrix):
    rows = matrix.shape[0]
    eighth = (33, N)
    dma = pltpu.SemaphoreType.DMA
    f32 = jnp.float32
    return pl.pallas_call(
        step_kernel,
        out_shape=jax.ShapeDtypeStruct(matrix.shape, f32),
        in_specs=[pl.BlockSpec(memory_space=pltpu.HBM)],
        out_specs=pl.BlockSpec(memory_space=pl.ANY),
        scratch_shapes=[
            pltpu.VMEM((rows, 2 * N), f32),
            pltpu.VMEM((2, rows, N), f32),
            pltpu.VMEM((2, EARLY, 2 * N), f32),
            pltpu.VMEM((2, EARLY, N), f32),
            pltpu.VMEM((CHUNKS, 3, QUARTER, N), f32),
            pltpu.VMEM((8, *eighth), f32),
            pltpu.VMEM((4, *eighth), f32),
            pltpu.VMEM((8, *eighth), f32),
            pltpu.VMEM((4, *eighth), f32),
            pltpu.VMEM((4, *eighth), f32),
            pltpu.VMEM((4, *eighth), f32),
            pltpu.VMEM((2 * N, 2 * N), f32),
            pltpu.VMEM((2, N, 2 * N), f32),
            ROUND_SCRATCH,
            [
                dma((LOADS,)),
                dma((14,)),
                dma,
                dma((4,)),
                dma((4,)),
                dma((4,)),
                dma((4,)),
                dma((2, RAW_PARTS)),
                dma((2, RAW_PARTS)),
                dma((2, 8)),
                dma((2, 8)),
                dma((2, CHUNKS)),
                dma((2, CHUNKS)),
                dma((CHUNKS, 4)),
                dma((CHUNKS, 4)),
                dma((CHUNKS, 4)),
                dma((CHUNKS, 4)),
                dma((2,)),
                pltpu.SemaphoreType.REGULAR,
                pltpu.SemaphoreType.REGULAR,
            ],
        ],
        compiler_params=pltpu.CompilerParams(collective_id=0, has_side_effects=True, vmem_limit_bytes=48 << 20),
        name="jacobi_step",
    )(matrix)


def solution(mesh):
    return jax.shard_map(
        per_device, mesh=mesh, in_specs=(P("row", "pair"),), out_specs=P("row", "pair"), check_vma=False
    )
```
